128 devices in a mesh: ex: 8 (over z, core), feat: 16 (over y, x).
Axes of the slice: x: 4, y: 4, z: 4, core: 2. Of those that a mesh axis runs over, the one named last changes fastest.
Arguments:
- lengths: int32 [2048], P(('ex', 'feat')), may hold values from 1 to 32, 40960 in all
- attn_in: bfloat16 [2048, 32, 4096], P(('ex', 'feat')), may hold values from -6 to 6
- context: bfloat16 [2048, 32, 4096], P(('ex', 'feat')), may hold values from -6 to 6
- grad_q: bfloat16 [2048, 32, 4096], P(('ex', 'feat')), may hold values from -6 to 6
- grad_k: bfloat16 [2048, 32, 1024], P(('ex', 'feat')), may hold values from -6 to 6
- grad_v: bfloat16 [2048, 32, 1024], P(('ex', 'feat')), may hold values from -6 to 6
- grad_o: bfloat16 [2048, 32, 4096], P(('ex', 'feat')), may hold values from -6 to 6
- proj_in: bfloat16 [4, 64, 4096], replicated, may hold values from -0.09375 to 0.09375
- proj_out_wide: bfloat16 [2, 64, 4096], replicated, may hold values from -0.09375 to 0.09375
- proj_out_narrow: bfloat16 [2, 64, 1024], replicated, may hold values from -0.1875 to 0.1875
- inv_hessian: float32 [4, 16, 256, 256], P(None, 'feat'), as said below
- query_feats: float32 [256, 4, 4096], P('ex', None, 'feat'), may hold values from -6 to 6
Outputs:
- scores: float32 [2048, 256], P(('ex', 'feat'))
The draws below stay inside these ranges and needn't reach their ends.
Inputs may be any that keep to these rules, and one draw needn't show every extreme that they name: `lengths`: each example's count of real tokens; some example has exactly 32. `inv_hessian`: each block is symmetric, and in each row the magnitudes off the diagonal sum to less than the diagonal entry.
All inputs are finite; a program needn't handle non-finite values. No bound on the sum of `lengths` on one device may be relied on, other than what follows from the above.
Results may differ from the reference program's by a relative error of at most 0.0041.
Values may be sent and summed in bfloat16 or wider, within the bound.
A program may use at most 128 MiB of HBM per device.

```python
import math
import jax
import jax.numpy as jnp
import numpy as np
from jax import lax

D = 4096
KVW = 1024
PR = 64
FM = 4096
HB = 256
KB = 16
LEN = 32
EX_DEV = 16
EXAMPLES = 2048
QUERIES = 256


def draw_inv_hessian(key, part):
    key = jax.random.fold_in(key, 5)
    key_diag, key_off = jax.random.split(key)
    diag = 1.0 + jax.random.uniform(key_diag, (4, KB, HB), jnp.float32)
    raw = jax.random.uniform(key_off, (4, KB, HB, HB), jnp.float32, -1.0, 1.0)
    sym = 0.5 * (raw + jnp.swapaxes(raw, 2, 3))
    rows = jnp.arange(HB, dtype=jnp.int32)
    eye = (rows[:, None] == rows[None, :]).astype(jnp.float32)
    block = sym * (0.9 / (HB - 1)) * (1.0 - eye) + eye * diag[:, :, :, None]
    level = jnp.arange(KB, dtype=jnp.float32) / max(KB - 1, 1)
    factor = jnp.exp(jnp.log(3.0) * level)
    return block * factor[None, :, None, None]


def shard_levels(own_key, dims, shards, low, largest):
    gain, own = 1.0, jax.random.fold_in(own_key, 6)
    for dim, blocks in shards:
        heights = jnp.exp(jax.random.uniform(jax.random.fold_in(own, dim), (blocks,), jnp.float32, low / len(shards), largest / len(shards)))
        gain = gain * jnp.repeat(heights, dims[dim] // blocks).reshape([-1 if axis == dim else 1 for axis in range(len(dims))])
    return gain


def length_profile(amount, total, reach, lean):
    portions = [(1 << 20) // math.isqrt(standing ** lean) + 1 for standing in range(2, amount + 1)]
    surplus, given = total - reach - (amount - 1), [1] * (amount - 1)
    while surplus > 0:
        candidates = [i for i in range(amount - 1) if given[i] < reach]
        whole, budget = sum([portions[i] for i in candidates]), surplus
        for i in candidates:
            extra = min(reach - given[i], max(1, budget * portions[i] // whole), surplus)
            given[i] = given[i] + extra
            surplus = surplus - extra
    return np.array([reach] + given)


def uneven_parts(key, number_of, total, most, lean):
    if number_of == 2:
        one = jax.random.randint(key, (), max(1, total - most), min(most, total - 1) + 1)
        return jnp.stack([one, total - one])
    tallies = jnp.asarray(length_profile(number_of, total, most, lean), jnp.int32)
    twos = (number_of - 1) // 2
    donor, sink = tallies[1:1 + 2 * twos:2], tallies[2:2 + 2 * twos:2]
    margin = jnp.minimum(donor - 1, most - sink)
    shifted = jax.random.randint(jax.random.fold_in(key, 1), (twos,), 0, 1 << 20) % (margin + 1)
    tallies = tallies.at[1:1 + 2 * twos:2].set(donor - shifted).at[2:2 + 2 * twos:2].set(sink + shifted)
    return tallies[jax.random.permutation(jax.random.fold_in(key, 2), number_of)]


def scatter_about(rng, shape, deviation, limit, pieces=(), held_as=jnp.bfloat16):
    factor_of = shard_levels(rng, shape, pieces, -0.22, 0.18) if pieces else 1.0
    drawn = jax.random.normal(rng, shape, jnp.float32) * deviation * factor_of
    return jnp.minimum(jnp.maximum(drawn, -limit), limit).astype(held_as)


def setup_inputs(seed: int = 0) -> dict:
    seeds = jax.random.split(jax.random.key(seed), 13)
    lengths = uneven_parts(seeds[0], EXAMPLES, EXAMPLES * LEN * 5 // 8, LEN, 0).astype(jnp.int32)
    attn_in = scatter_about(seeds[1], (EXAMPLES, LEN, D), 1.0, 6.0, ((0, 128),))
    context = scatter_about(seeds[2], (EXAMPLES, LEN, D), 1.0, 6.0, ((0, 128),))
    grad_q = scatter_about(seeds[3], (EXAMPLES, LEN, D), 1.0, 6.0, ((0, 128),))
    grad_k = scatter_about(seeds[4], (EXAMPLES, LEN, KVW), 1.0, 6.0, ((0, 128),))
    grad_v = scatter_about(seeds[5], (EXAMPLES, LEN, KVW), 1.0, 6.0, ((0, 128),))
    grad_o = scatter_about(seeds[6], (EXAMPLES, LEN, D), 1.0, 6.0, ((0, 128),))
    proj_in = scatter_about(seeds[7], (4, PR, D), D ** -0.5, 0.09375)
    proj_out_wide = scatter_about(seeds[8], (2, PR, D), D ** -0.5, 0.09375)
    proj_out_narrow = scatter_about(seeds[9], (2, PR, KVW), KVW ** -0.5, 0.1875)
    inv_hessian = draw_inv_hessian(jax.random.fold_in(seeds[12], 71), 0)
    query_feats = scatter_about(seeds[11], (QUERIES, 4, FM), 1.0, 6.0, ((0, 8), (2, 16)), jnp.float32)
    return dict(lengths=lengths, attn_in=attn_in, context=context, grad_q=grad_q, grad_k=grad_k, grad_v=grad_v, grad_o=grad_o, proj_in=proj_in, proj_out_wide=proj_out_wide, proj_out_narrow=proj_out_narrow, inv_hessian=inv_hessian, query_feats=query_feats)


def example_features(lengths, attn_in, context, grad_q, grad_k, grad_v, grad_o, proj_in, proj_out_wide, proj_out_narrow):
    count = lengths.shape[0]
    positions = jnp.arange(LEN, dtype=jnp.int32)
    keep = (positions[None, :] < lengths[:, None]).astype(jnp.float32)[:, :, None]
    sources = (attn_in, attn_in, attn_in, context)
    targets = (grad_q, grad_k, grad_v, grad_o)
    outside = (proj_out_wide[0], proj_out_narrow[0], proj_out_narrow[1], proj_out_wide[1])
    blocks = []
    for matrix in range(4):
        source = sources[matrix].reshape(count * LEN, -1)
        target = targets[matrix].reshape(count * LEN, -1)
        in_proj = jnp.dot(source, proj_in[matrix].T, preferred_element_type=jnp.float32).reshape(count, LEN, PR)
        in_proj = (in_proj * keep).astype(jnp.bfloat16)
        out_proj = jnp.dot(target, outside[matrix].T, preferred_element_type=jnp.float32).reshape(count, LEN, PR)
        out_proj = (out_proj * keep).astype(jnp.bfloat16)
        grads = jnp.einsum('eti,etj->eij', out_proj.astype(jnp.float32), in_proj.astype(jnp.float32), precision=lax.Precision.HIGHEST)
        blocks.append(grads.reshape(count, FM))
    return jnp.stack(blocks, axis=1)

def reference(lengths, attn_in, context, grad_q, grad_k, grad_v, grad_o, proj_in, proj_out_wide, proj_out_narrow, inv_hessian, query_feats):
    groups = EXAMPLES // EX_DEV

    def one_group(items):
        return example_features(items[0], items[1], items[2], items[3], items[4], items[5], items[6], proj_in, proj_out_wide, proj_out_narrow)
    grads = lax.map(one_group, (lengths.reshape(groups, EX_DEV), attn_in.reshape(groups, EX_DEV, LEN, D), context.reshape(groups, EX_DEV, LEN, D), grad_q.reshape(groups, EX_DEV, LEN, D), grad_k.reshape(groups, EX_DEV, LEN, KVW), grad_v.reshape(groups, EX_DEV, LEN, KVW), grad_o.reshape(groups, EX_DEV, LEN, D)))
    grads = grads.reshape(EXAMPLES, 4, KB, HB)
    precond = jnp.einsum('emkf,mkfg->emkg', grads, inv_hessian, precision=lax.Precision.HIGHEST)
    precond = precond.reshape(EXAMPLES, 4 * FM)
    self_inf = lax.optimization_barrier(jnp.sum(precond * grads.reshape(EXAMPLES, 4 * FM), axis=1))
    raw = jnp.dot(precond, query_feats.reshape(QUERIES, 4 * FM).T, precision=lax.Precision.HIGHEST)
    return raw * lax.rsqrt(self_inf + 1e-06)[:, None]
```

```python
import functools

import jax
import jax.numpy as jnp
from jax import lax
from jax.experimental import pallas as pl
from jax.experimental.pallas import tpu as pltpu
from jax.sharding import PartitionSpec as P

MESH = pl.DeviceIdType.MESH
NT = (((1,), (1,)), ((), ()))
BF = jnp.bfloat16
F32 = jnp.float32

D = 4096
KVW = 1024
PR = 64
HB = 256
LEN = 32
EXD = 16
ROWS = EXD * LEN
OWN = 16
EXN = 8
QL = 32
QN = 256
RC = 256
NC = ROWS // RC
W = 384


def kernel(
    len_ref, xa, xc, gq, gk, gv, go, win, wwide, wnar, hes, qry, out_ref,
    xa_v, xc_v, gq_v, gk_v, gv_v, go_v, win_v, wwide_v, wnar_v, hes_v, qry_v,
    hb_v, ploc, pall, pin, pin_o, ot, mask_v, g32, gsend, grec, acc, tacc, sbuf, srec,
    load_sem, p_send, p_recv, g_send, g_recv, s_send, s_recv,
):
    ex = lax.axis_index("ex")
    ft = lax.axis_index("feat")
    fy, fx = ft // 4, ft % 4

    def peer(s):
        return ((fy + s // 4) % 4) * 4 + (fx + s % 4) % 4

    loads = {}

    def load(name, src, dst):
        copy = pltpu.make_async_copy(src, dst, load_sem.at[len(loads)])
        copy.start()
        loads[name] = copy

    load("hes", hes.at[:, 0], hes_v)
    load("qry", qry, qry_v)
    for m in range(3):
        load(f"win{m}", win.at[m], win_v.at[pl.ds(m * PR, PR)])
    for c in range(NC):
        load(f"xa{c}", xa.at[pl.ds(c * RC, RC)], xa_v.at[pl.ds(c * RC, RC)])
    load("wnar", wnar, wnar_v)
    for c in range(NC):
        load(f"gk{c}", gk.at[pl.ds(c * RC, RC)], gk_v.at[pl.ds(c * RC, RC)])
    for c in range(NC):
        load(f"gv{c}", gv.at[pl.ds(c * RC, RC)], gv_v.at[pl.ds(c * RC, RC)])
    load("wq", wwide.at[0], wwide_v.at[0])
    for c in range(NC):
        load(f"gq{c}", gq.at[pl.ds(c * RC, RC)], gq_v.at[pl.ds(c * RC, RC)])
    load("win3", win.at[3], win_v.at[pl.ds(4 * PR, PR)])
    for c in range(NC):
        load(f"xc{c}", xc.at[pl.ds(c * RC, RC)], xc_v.at[pl.ds(c * RC, RC)])
    load("wo", wwide.at[1], wwide_v.at[1])
    for c in range(NC):
        load(f"go{c}", go.at[pl.ds(c * RC, RC)], go_v.at[pl.ds(c * RC, RC)])

    barrier = pltpu.get_barrier_semaphore()

    @pl.loop(1, OWN)
    def _(s):
        pl.semaphore_signal(barrier, inc=1, device_id={"feat": peer(s)}, device_id_type=MESH)

    @pl.loop(1, EXN)
    def _(s):
        pl.semaphore_signal(barrier, inc=1, device_id={"ex": (ex + s) % EXN}, device_id_type=MESH)

    lane = lax.broadcasted_iota(jnp.int32, (16, 256), 1)
    lane_e = (lane // LEN) % 4
    lane_t = lane % LEN
    for e in range(EXD):
        on = (lane_e == e % 4) & (lane_t < len_ref[e])
        mask_v[e * 16:(e + 1) * 16, :] = jnp.where(on, 1.0, 0.0).astype(BF)

    loads["hes"].wait()
    loads["qry"].wait()
    for m in range(4):
        ploc[m] = jnp.dot(
            qry_v[:, m, :], hes_v[m], preferred_element_type=F32, precision=lax.Precision.HIGHEST
        ).astype(BF)
        hb_v[m] = hes_v[m].astype(BF)

    pl.semaphore_wait(barrier, OWN - 1 + EXN - 1)

    my_q = pl.ds(pl.multiple_of(ex * QL, QL), QL)

    def p_copy(s):
        return pltpu.make_async_remote_copy(
            src_ref=ploc, dst_ref=pall.at[:, my_q, :], send_sem=p_send, recv_sem=p_recv,
            device_id={"ex": (ex + s) % EXN}, device_id_type=MESH,
        )

    @pl.loop(1, EXN)
    def _(s):
        p_copy(s).start()

    pall[:, my_q, :] = ploc[...]

    half = lax.broadcasted_iota(jnp.int32, (128, 128), 1) < PR
    my_rows = pl.ds(pl.multiple_of(ft * EXD, EXD), EXD)

    def rows_of(k):
        return pl.ds(pl.multiple_of(k * EXD, EXD), EXD)

    def g_copy(m, s):
        to = peer(s)
        return pltpu.make_async_remote_copy(
            src_ref=gsend.at[m, rows_of(to), :], dst_ref=grec.at[m, my_rows, :],
            send_sem=g_send.at[m], recv_sem=g_recv.at[m],
            device_id={"feat": to}, device_id_type=MESH,
        )

    def outer(m, c, target_v, weight, pair, dup):
        rows = pl.ds(c * RC, RC)
        o_t = lax.dot_general(weight, target_v[rows, :], NT, preferred_element_type=F32)
        for b in range(RC // 128):
            ot[b] = o_t[:, b * 128:(b + 1) * 128]
        for b in range(RC // 128):
            g = c * (RC // 128) + b
            parts = [
                [ot[b, pl.ds(2 * ih + il, 16, stride=4), :].astype(BF) for il in range(2)]
                for ih in range(2)
            ]
            lhs = jnp.concatenate([jnp.concatenate(p, axis=1) for p in parts], axis=0)
            blocks = []
            for e in range(4):
                mk = mask_v[(4 * g + e) * 16:(4 * g + e + 1) * 16, :]
                blocks.append(lhs * jnp.concatenate([mk, mk], axis=0))
            lhs = jnp.concatenate(blocks, axis=0)
            top, bottom = pair(g)
            rhs = jnp.concatenate([top, bottom], axis=0)
            r = jnp.dot(lhs, rhs, preferred_element_type=F32)
            for e in range(4):
                for ih in range(2):
                    at = (2 * e + ih) * 16
                    g32[ih, pl.ds(4 * g + e, 16, stride=16), :] = r[at:at + 16, :]

    def finish(m):
        gsend[m] = jnp.concatenate([g32[0], g32[1]], axis=1).astype(BF)

        @pl.loop(1, OWN)
        def _(s):
            g_copy(m, s).start()

        grec[m, my_rows, :] = gsend[m, my_rows, :]

    def split(x, left):
        turned = pltpu.roll(x, PR, axis=1)
        on_left, on_right = (x, turned) if left else (turned, x)
        return jnp.where(half, on_left, 0.0).astype(BF), jnp.where(half, 0.0, on_right).astype(BF)

    def group(g):
        return pl.ds(g * 128, 128)

    for m in range(3):
        loads[f"win{m}"].wait()
    win_v[pl.ds(3 * PR, PR), :] = win_v[pl.ds(2 * PR, PR), :]
    for c in range(NC):
        loads[f"xa{c}"].wait()
        pin[c * RC:(c + 1) * RC, :] = lax.dot_general(
            xa_v[c * RC:(c + 1) * RC, :], win_v[0:4 * PR, :], NT, preferred_element_type=F32
        )

    def pair_q(g):
        return split(pin[group(g), 0:128], True)

    def pair_k(g):
        return split(pin[group(g), 0:128], False)

    def pair_v(g):
        x = pin[group(g), 128:256]
        return jnp.where(half, x, 0.0).astype(BF), jnp.where(half, 0.0, x).astype(BF)

    def pair_o(g):
        x = pin_o[group(g), :]
        return jnp.where(half, x, 0.0).astype(BF), jnp.where(half, 0.0, x).astype(BF)

    loads["wnar"].wait()
    for c in range(NC):
        loads[f"gk{c}"].wait()
        outer(1, c, gk_v, wnar_v[0], pair_k, False)
    finish(1)
    for c in range(NC):
        loads[f"gv{c}"].wait()
        outer(2, c, gv_v, wnar_v[1], pair_v, True)
    finish(2)
    loads["wq"].wait()
    for c in range(NC):
        loads[f"gq{c}"].wait()
        outer(0, c, gq_v, wwide_v[0], pair_q, False)
    finish(0)
    loads["win3"].wait()
    win_v[pl.ds(5 * PR, PR), :] = win_v[pl.ds(4 * PR, PR), :]
    for c in range(NC):
        loads[f"xc{c}"].wait()
        pin_o[c * RC:(c + 1) * RC, :] = lax.dot_general(
            xc_v[c * RC:(c + 1) * RC, :], win_v[4 * PR:6 * PR, :], NT, preferred_element_type=F32
        )
    loads["wo"].wait()
    for c in range(NC):
        loads[f"go{c}"].wait()
        outer(3, c, go_v, wwide_v[1], pair_o, True)
    finish(3)

    others = (OWN - 1) * EXD
    pltpu.make_async_copy(
        pall.at[:, pl.ds(0, QN - QL), :], pall.at[:, pl.ds(0, QN - QL), :], p_recv
    ).wait()
    order = (1, 2, 0, 3)
    for i, m in enumerate(order):
        pltpu.make_async_copy(
            grec.at[m, pl.ds(0, others), :], grec.at[m, pl.ds(0, others), :], g_recv.at[m]
        ).wait()
        got = grec[m]
        raw = lax.dot_general(got, pall[m], NT, preferred_element_type=F32)
        own = jnp.dot(got, hb_v[m], preferred_element_type=F32) * got.astype(F32)
        own = own[:, 0:128] + own[:, 128:256]
        if i == 0:
            acc[...] = raw
            tacc[...] = own
        elif i < 3:
            acc[...] += raw
            tacc[...] += own
        else:
            raw = acc[...] + raw
            own = tacc[...] + own
            own = own + pltpu.roll(own, 64, axis=1)
            high = own.astype(BF).astype(F32)
            lanes = lax.broadcasted_iota(jnp.int32, (OWN * EXD, 128), 1)
            own = jnp.where(lanes < 64, high, own - high)
            sbuf[:, 0:QN] = raw.astype(BF)
            sbuf[:, QN:W] = own.astype(BF)

    def s_copy(s):
        to = peer(s)
        return pltpu.make_async_remote_copy(
            src_ref=sbuf.at[rows_of(to), :], dst_ref=srec.at[my_rows, :],
            send_sem=s_send, recv_sem=s_recv, device_id={"feat": to}, device_id_type=MESH,
        )

    @pl.loop(1, OWN)
    def _(s):
        s_copy(s).start()

    srec[my_rows, :] = sbuf[my_rows, :]
    pltpu.make_async_copy(
        srec.at[pl.ds(0, others), :], srec.at[pl.ds(0, others), :], s_recv
    ).wait()
    total = srec[0:EXD, :].astype(F32)
    for s in range(1, OWN):
        total = total + srec[s * EXD:(s + 1) * EXD, :].astype(F32)
    self_inf = jnp.sum(total[:, QN:W], axis=1, keepdims=True)
    out_ref[...] = total[:, 0:QN] * lax.rsqrt(self_inf + 1e-06)

    for m in range(4):
        pltpu.make_async_copy(
            gsend.at[m, pl.ds(0, others), :], gsend.at[m, pl.ds(0, others), :], g_send.at[m]
        ).wait()
    pltpu.make_async_copy(
        sbuf.at[pl.ds(0, others), :], sbuf.at[pl.ds(0, others), :], s_send
    ).wait()
    pltpu.make_async_copy(
        pall.at[:, pl.ds(0, QN - QL), :], pall.at[:, pl.ds(0, QN - QL), :], p_send
    ).wait()


def per_device(
    lengths, attn_in, context, grad_q, grad_k, grad_v, grad_o,
    proj_in, proj_out_wide, proj_out_narrow, inv_hessian, query_feats,
):
    def flat(x):
        return x.reshape(ROWS, x.shape[-1])

    any_space = pl.BlockSpec(memory_space=pl.ANY)
    dma = pltpu.SemaphoreType.DMA
    return pl.pallas_call(
        kernel,
        out_shape=jax.ShapeDtypeStruct((EXD, QN), F32),
        in_specs=[pl.BlockSpec(memory_space=pltpu.SMEM)] + [any_space] * 11,
        out_specs=pl.BlockSpec(memory_space=pltpu.VMEM),
        scratch_shapes=[
            pltpu.VMEM((ROWS, D), BF),
            pltpu.VMEM((ROWS, D), BF),
            pltpu.VMEM((ROWS, D), BF),
            pltpu.VMEM((ROWS, KVW), BF),
            pltpu.VMEM((ROWS, KVW), BF),
            pltpu.VMEM((ROWS, D), BF),
            pltpu.VMEM((6 * PR, D), BF),
            pltpu.VMEM((2, PR, D), BF),
            pltpu.VMEM((2, PR, KVW), BF),
            pltpu.VMEM((4, HB, HB), F32),
            pltpu.VMEM((QL, 4, HB), F32),
            pltpu.VMEM((4, HB, HB), BF),
            pltpu.VMEM((4, QL, HB), BF),
            pltpu.VMEM((4, QN, HB), BF),
            pltpu.VMEM((ROWS, 256), F32),
            pltpu.VMEM((ROWS, 128), F32),
            pltpu.VMEM((RC // 128, PR, 128), F32),
            pltpu.VMEM((EXD * 16, 256), BF),
            pltpu.VMEM((2, OWN * EXD, 128), F32),
            pltpu.VMEM((4, OWN * EXD, HB), BF),
            pltpu.VMEM((4, OWN * EXD, HB), BF),
            pltpu.VMEM((OWN * EXD, QN), F32),
            pltpu.VMEM((OWN * EXD, 128), F32),
            pltpu.VMEM((OWN * EXD, W), BF),
            pltpu.VMEM((OWN * EXD, W), BF),
            dma((40,)),
            dma,
            dma,
            dma((4,)),
            dma((4,)),
            dma,
            dma,
        ],
        compiler_params=pltpu.CompilerParams(
            collective_id=0, has_side_effects=True, vmem_limit_bytes=56 << 20
        ),
    )(
        lengths, flat(attn_in), flat(context), flat(grad_q), flat(grad_k), flat(grad_v),
        flat(grad_o), proj_in, proj_out_wide, proj_out_narrow, inv_hessian, query_feats,
    )


def solution(mesh):
    both = P(("ex", "feat"), None, None)
    in_specs = (
        P(("ex", "feat")), both, both, both, both, both, both,
        P(), P(), P(),
        P(None, "feat", None, None),
        P("ex", None, "feat"),
    )
    return jax.shard_map(
        per_device, mesh=mesh, in_specs=in_specs, out_specs=P(("ex", "feat"), None), check_vma=False
    )
```

```python
import jax
import jax.numpy as jnp
from jax import lax
from jax.experimental import pallas as pl
from jax.experimental.pallas import tpu as pltpu
from jax.sharding import PartitionSpec as P

MESH = pl.DeviceIdType.MESH
NT = (((1,), (1,)), ((), ()))
BF = jnp.bfloat16
F32 = jnp.float32

D = 4096
KVW = 1024
PR = 64
HB = 256
LEN = 32
EXD = 16
ROWS = EXD * LEN
SIDE = 4
OWN = SIDE * SIDE
EXN = 8
QL = 32
QN = 256
W = 384
PITCH = 17
QUERY, KEY, VALUE, OUTPUT = range(4)


def hops(s):
    dy, dx = divmod(s, SIDE)
    return min(dy, SIDE - dy) + min(dx, SIDE - dx)


SLOTS = sorted(range(OWN), key=hops)
GROUPS = [[i for i in range(OWN) if max(hops(SLOTS[i]), 1) == h] for h in range(1, SIDE + 1)]
GROUP_OF = {i: n for n, g in enumerate(GROUPS) for i in g}
FAR_FIRST = range(OWN - 1, 0, -1)


def arrived(ref, sem):
    pltpu.make_async_copy(ref, ref, sem).wait()


def kernel(
    len_ref, xa, xc, gq, gk, gv, go, win, wwide, wnar, hes, qry, out_ref,
    xa_v, xc_v, gq_v, gk_v, gv_v, go_v, win_v, wwide_v, wnar_v, hes_v, qry_v,
    hb_v, ploc, pall, pin, pin_o, ot, mask_v, g32, gsend, grec, acc, tacc, sbuf, srec,
    load_sem, p_send, p_recv, g_send, g_recv, s_send, s_recv,
):
    ex = lax.axis_index("ex")
    ft = lax.axis_index("feat")
    fy, fx = ft // SIDE, ft % SIDE

    def ahead(i):
        dy, dx = divmod(SLOTS[i], SIDE)
        return ((fy + dy) % SIDE) * SIDE + (fx + dx) % SIDE

    def behind(i):
        dy, dx = divmod(SLOTS[i], SIDE)
        return ((fy + SIDE - dy) % SIDE) * SIDE + (fx + SIDE - dx) % SIDE

    loads = {}
    waited = set()

    def load(name, src, dst):
        copy = pltpu.make_async_copy(src, dst, load_sem.at[len(loads)])
        copy.start()
        loads[name] = copy

    def ready(*names):
        for name in names:
            loads[name].wait()
            waited.add(name)

    def load_rows(name, src, dst, at, size):
        load(name, src.at[pl.ds(at, size)], dst.at[pl.ds(at, size)])

    load("hes", hes.at[:, 0], hes_v)
    load("qry", qry, qry_v)
    load("wnar", wnar, wnar_v)
    load("gk", gk, gk_v)
    load("gv", gv, gv_v)
    load("win", win.at[pl.ds(0, 3)], win_v.at[pl.ds(0, 3)])
    load_rows("xa0", xa, xa_v, 0, 256)
    load_rows("xa1", xa, xa_v, 256, 256)
    load("wq", wwide.at[0], wwide_v.at[0])
    load_rows("gq0", gq, gq_v, 0, 256)
    load_rows("gq1", gq, gq_v, 256, 256)
    load("win3", win.at[3], win_v.at[4])
    load_rows("xc0", xc, xc_v, 0, 256)
    load_rows("xc1", xc, xc_v, 256, 256)
    load("wo", wwide.at[1], wwide_v.at[1])
    load_rows("go0", go, go_v, 0, 256)
    load_rows("go1", go, go_v, 256, 128)
    load_rows("go2", go, go_v, 384, 128)

    barrier = pltpu.get_barrier_semaphore()
    for i in FAR_FIRST:
        pl.semaphore_signal(barrier, inc=1, device_id={"feat": ahead(i)}, device_id_type=MESH)
    for s in range(1, EXN):
        pl.semaphore_signal(barrier, inc=1, device_id={"ex": (ex + s) % EXN}, device_id_type=MESH)

    lane = lax.broadcasted_iota(jnp.int32, (16, 256), 1)
    lane_e = (lane // LEN) % 4
    lane_t = lane % LEN
    for e in range(EXD):
        on = (lane_e == e % 4) & (lane_t < len_ref[e])
        mask_v[e * 16:(e + 1) * 16, :] = jnp.where(on, 1.0, 0.0).astype(BF)

    def halves(x):
        high = x.astype(BF)
        return high, (x - high.astype(F32)).astype(BF)

    ready("hes", "qry")
    for m in range(4):
        q_high, q_low = halves(qry_v[:, m, :])
        h_high, h_low = halves(hes_v[m])
        hb_v[m] = h_high
        both = jnp.dot(
            jnp.concatenate([q_high, q_low], axis=0), h_high, preferred_element_type=F32
        )
        rest = jnp.dot(q_high, h_low, preferred_element_type=F32)
        ploc[m] = (both[0:QL] + (both[QL:2 * QL] + rest)).astype(BF)

    pl.semaphore_wait(barrier, OWN - 1 + EXN - 1)

    my_q = pl.ds(pl.multiple_of(ex * QL, QL), QL)
    for s in range(1, EXN):
        pltpu.make_async_remote_copy(
            src_ref=ploc, dst_ref=pall.at[:, my_q, :], send_sem=p_send, recv_sem=p_recv,
            device_id={"ex": (ex + s) % EXN}, device_id_type=MESH,
        ).start()
    pall[:, my_q, :] = ploc[...]

    half = lax.broadcasted_iota(jnp.int32, (128, 128), 1) < PR

    def rows_of(k):
        return pl.ds(pl.multiple_of(k * EXD, EXD), EXD)

    def project(m, target_v, weight, first, count):
        o_t = lax.dot_general(
            weight, target_v[first:first + count, :], NT, preferred_element_type=F32
        )
        for b in range(count // 128):
            ot[m, first // 128 + b] = o_t[:, b * 128:(b + 1) * 128]

    def split(x, left, twice):
        turned = x if twice else pltpu.roll(x, PR, axis=1)
        on_left, on_right = (x, turned) if left else (turned, x)
        return jnp.where(half, on_left, 0.0).astype(BF), jnp.where(half, 0.0, on_right).astype(BF)

    def pair(m, g):
        rows = pl.ds(g * 128, 128)
        if m == QUERY:
            return split(pin[rows, 0:128], True, False)
        if m == KEY:
            return split(pin[rows, 0:128], False, False)
        if m == VALUE:
            return split(pin[rows, 128:256], True, True)
        return split(pin_o[rows, :], True, True)

    def outer(m, g):
        parts = [
            [ot[m, g, pl.ds(2 * ih + il, 16, stride=4), :].astype(BF) for il in range(2)]
            for ih in range(2)
        ]
        lhs = jnp.concatenate([jnp.concatenate(p, axis=1) for p in parts], axis=0)
        blocks = []
        for e in range(4):
            mk = mask_v[(4 * g + e) * 16:(4 * g + e + 1) * 16, :]
            blocks.append(lhs * jnp.concatenate([mk, mk], axis=0))
        lhs = jnp.concatenate(blocks, axis=0)
        rhs = jnp.concatenate(pair(m, g), axis=0)
        r = jnp.dot(lhs, rhs, preferred_element_type=F32)
        for e in range(4):
            for ih in range(2):
                at = (2 * e + ih) * 16
                g32[m, ih, pl.ds(4 * g + e, 16, stride=PITCH), :] = r[at:at + 16, :]

    def gather(m):
        for k in range(OWN):
            gsend[m, k * EXD:(k + 1) * EXD, :] = jnp.concatenate(
                [g32[m, ih, k * PITCH:k * PITCH + EXD, :] for ih in range(2)], axis=1
            ).astype(BF)

    def send(m):
        for i in FAR_FIRST:
            to = ahead(i)
            pltpu.make_async_remote_copy(
                src_ref=gsend.at[m, rows_of(to), :],
                dst_ref=grec.at[m, pl.ds(i * EXD, EXD), :],
                send_sem=g_send, recv_sem=g_recv.at[m if m < OUTPUT else OUTPUT + GROUP_OF[i]],
                device_id={"feat": to}, device_id_type=MESH,
            ).start()
        grec[m, 0:EXD, :] = gsend[m, rows_of(ft), :]

    def project_in(dst, source_v, weight, first, count):
        dst[first:first + count, :] = lax.dot_general(
            source_v[first:first + count, :], weight, NT, preferred_element_type=F32
        )

    ready("wnar", "gk", "gv")
    project(KEY, gk_v, wnar_v[0], 0, ROWS)
    project(VALUE, gv_v, wnar_v[1], 0, ROWS)
    ready("win", "xa0")
    win_v[3] = win_v[2]
    w_qkvv = win_v[0:4].reshape(4 * PR, D)
    project_in(pin, xa_v, w_qkvv, 0, 256)
    ready("xa1")
    project_in(pin, xa_v, w_qkvv, 256, 256)
    for g in (0, 1):
        outer(KEY, g)
        outer(VALUE, g)
    ready("wq", "gq0")
    project(QUERY, gq_v, wwide_v[0], 0, 256)
    for g in (2, 3):
        outer(KEY, g)
        outer(VALUE, g)
    gather(KEY)
    gather(VALUE)
    send(KEY)
    send(VALUE)
    ready("gq1")
    project(QUERY, gq_v, wwide_v[0], 256, 256)
    for g in (0, 1):
        outer(QUERY, g)
    ready("win3", "xc0")
    win_v[5] = win_v[4]
    w_oo = win_v[4:6].reshape(2 * PR, D)
    project_in(pin_o, xc_v, w_oo, 0, 256)
    for g in (2, 3):
        outer(QUERY, g)
    gather(QUERY)
    send(QUERY)
    ready("xc1")
    project_in(pin_o, xc_v, w_oo, 256, 256)
    ready("wo", "go0")
    project(OUTPUT, go_v, wwide_v[1], 0, 256)
    ready("go1")
    project(OUTPUT, go_v, wwide_v[1], 256, 128)
    for g in (0, 1):
        outer(OUTPUT, g)
    ready("go2")
    project(OUTPUT, go_v, wwide_v[1], 384, 128)
    outer(OUTPUT, 2)
    outer(OUTPUT, 3)
    gather(OUTPUT)
    send(OUTPUT)

    others = (OWN - 1) * EXD

    def products(m, rows):
        got = grec[m, rows, :]
        raw = lax.dot_general(got, pall[m], NT, preferred_element_type=F32)
        own = jnp.dot(got, hb_v[m], preferred_element_type=F32) * got.astype(F32)
        return raw, own[:, 0:128] + own[:, 128:256]

    arrived(pall.at[:, pl.ds(0, QN - QL), :], p_recv)
    for m in (KEY, VALUE, QUERY):
        arrived(grec.at[m, pl.ds(0, others), :], g_recv.at[m])
        raw, own = products(m, slice(0, OWN * EXD))
        if m == KEY:
            acc[...] = raw
            tacc[...] = own
        else:
            acc[...] += raw
            tacc[...] += own

    for n, group in enumerate(GROUPS):
        partners = [i for i in group if i > 0]
        arrived(grec.at[OUTPUT, pl.ds(0, len(partners) * EXD), :], g_recv.at[OUTPUT + n])
        rows = slice(group[0] * EXD, (group[-1] + 1) * EXD)
        raw, own = products(OUTPUT, rows)
        raw = raw + acc[rows, :]
        own = own + tacc[rows, :]
        own = own + pltpu.roll(own, 64, axis=1)
        high = own.astype(BF).astype(F32)
        left = lax.broadcasted_iota(jnp.int32, own.shape, 1) < 64
        sbuf[rows, 0:QN] = raw.astype(BF)
        sbuf[rows, QN:W] = jnp.where(left, high, own - high).astype(BF)
        for i in partners:
            at = pl.ds(i * EXD, EXD)
            pltpu.make_async_remote_copy(
                src_ref=sbuf.at[at, :], dst_ref=srec.at[at, :], send_sem=s_send,
                recv_sem=s_recv.at[n], device_id={"feat": behind(i)}, device_id_type=MESH,
            ).start()

    total = sbuf[0:EXD, :].astype(F32)
    for n, group in enumerate(GROUPS):
        partners = [i for i in group if i > 0]
        arrived(srec.at[pl.ds(0, len(partners) * EXD), :], s_recv.at[n])
        for i in partners:
            total = total + srec[i * EXD:(i + 1) * EXD, :].astype(F32)
    self_inf = jnp.sum(total[:, QN:W], axis=1, keepdims=True)
    out_ref[...] = total[:, 0:QN] * lax.rsqrt(self_inf + 1e-06)

    arrived(gsend.at[:, pl.ds(0, others), :], g_send)
    arrived(sbuf.at[pl.ds(0, others), :], s_send)
    arrived(pall.at[:, pl.ds(0, QN - QL), :], p_send)


def per_device(
    lengths, attn_in, context, grad_q, grad_k, grad_v, grad_o,
    proj_in, proj_out_wide, proj_out_narrow, inv_hessian, query_feats,
):
    def flat(x):
        return x.reshape(ROWS, x.shape[-1])

    any_space = pl.BlockSpec(memory_space=pl.ANY)
    dma = pltpu.SemaphoreType.DMA
    return pl.pallas_call(
        kernel,
        out_shape=jax.ShapeDtypeStruct((EXD, QN), F32),
        in_specs=[pl.BlockSpec(memory_space=pltpu.SMEM)] + [any_space] * 11,
        out_specs=pl.BlockSpec(memory_space=pltpu.VMEM),
        scratch_shapes=[
            pltpu.VMEM((ROWS, D), BF),
            pltpu.VMEM((ROWS, D), BF),
            pltpu.VMEM((ROWS, D), BF),
            pltpu.VMEM((ROWS, KVW), BF),
            pltpu.VMEM((ROWS, KVW), BF),
            pltpu.VMEM((ROWS, D), BF),
            pltpu.VMEM((6, PR, D), BF),
            pltpu.VMEM((2, PR, D), BF),
            pltpu.VMEM((2, PR, KVW), BF),
            pltpu.VMEM((4, HB, HB), F32),
            pltpu.VMEM((QL, 4, HB), F32),
            pltpu.VMEM((4, HB, HB), BF),
            pltpu.VMEM((4, QL, HB), BF),
            pltpu.VMEM((4, QN, HB), BF),
            pltpu.VMEM((ROWS, 256), F32),
            pltpu.VMEM((ROWS, 128), F32),
            pltpu.VMEM((4, EXD // 4, PR, 128), F32),
            pltpu.VMEM((EXD * 16, 256), BF),
            pltpu.VMEM((4, 2, OWN * PITCH, 128), F32),
            pltpu.VMEM((4, OWN * EXD, HB), BF),
            pltpu.VMEM((4, OWN * EXD, HB), BF),
            pltpu.VMEM((OWN * EXD, QN), F32),
            pltpu.VMEM((OWN * EXD, 128), F32),
            pltpu.VMEM((OWN * EXD, W), BF),
            pltpu.VMEM((OWN * EXD, W), BF),
            dma((18,)),
            dma,
            dma,
            dma,
            dma((OUTPUT + len(GROUPS),)),
            dma,
            dma((len(GROUPS),)),
        ],
        compiler_params=pltpu.CompilerParams(
            collective_id=0, has_side_effects=True, vmem_limit_bytes=56 << 20
        ),
    )(
        lengths, flat(attn_in), flat(context), flat(grad_q), flat(grad_k), flat(grad_v),
        flat(grad_o), proj_in, proj_out_wide, proj_out_narrow, inv_hessian, query_feats,
    )


def solution(mesh):
    both = P(("ex", "feat"), None, None)
    in_specs = (
        P(("ex", "feat")), both, both, both, both, both, both,
        P(), P(), P(),
        P(None, "feat", None, None),
        P("ex", None, "feat"),
    )
    return jax.shard_map(
        per_device, mesh=mesh, in_specs=in_specs, out_specs=P(("ex", "feat"), None), check_vma=False
    )
```

```python
import jax
import jax.numpy as jnp
from jax import lax
from jax.experimental import pallas as pl
from jax.experimental.pallas import tpu as pltpu
from jax.sharding import PartitionSpec as P

MESH = pl.DeviceIdType.MESH
NT = (((1,), (1,)), ((), ()))
BF = jnp.bfloat16
F32 = jnp.float32

D = 4096
KVW = 1024
PR = 64
HB = 256
LEN = 32
EXD = 16
ROWS = EXD * LEN
SIDE = 4
OWN = SIDE * SIDE
EXN = 8
QL = 32
QN = 256
W = 384
RC = 256
PITCH = 17
QUERY, KEY, VALUE, OUTPUT = range(4)


def hops(s):
    dy, dx = divmod(s, SIDE)
    return min(dy, SIDE - dy) + min(dx, SIDE - dx)


SLOTS = sorted(range(OWN), key=hops)
GROUPS = [[i for i in range(OWN) if max(hops(SLOTS[i]), 1) == h] for h in range(1, SIDE + 1)]
GROUP_OF = {i: n for n, g in enumerate(GROUPS) for i in g}
FAR_FIRST = range(OWN - 1, 0, -1)


def arrived(ref, sem):
    pltpu.make_async_copy(ref, ref, sem).wait()


def kernel(
    lengths, xa, xc, gq, gk, gv, go, win, wwide, wnar, hes, qry, out_ref,
    len_ref, xa_v, xc_v, gq_v, gk_v, gv_v, go_v, win_v, wwide_v, wnar_v, hes_v, qry_v,
    hb_v, ploc, pall, pin, pin_o, ot, mask_v, g32, gsend, grec, acc, tacc, sbuf, srec,
    load_sem, p_send, p_recv, g_send, g_recv, s_send, s_recv,
):
    ex = lax.axis_index("ex")
    ft = lax.axis_index("feat")
    fy, fx = ft // SIDE, ft % SIDE

    def ahead(i):
        dy, dx = divmod(SLOTS[i], SIDE)
        return ((fy + dy) % SIDE) * SIDE + (fx + dx) % SIDE

    def behind(i):
        dy, dx = divmod(SLOTS[i], SIDE)
        return ((fy + SIDE - dy) % SIDE) * SIDE + (fx + SIDE - dx) % SIDE

    loads = {}
    waited = set()

    def load(name, src, dst):
        copy = pltpu.make_async_copy(src, dst, load_sem.at[len(loads)])
        copy.start()
        loads[name] = copy

    def ready(*names):
        for name in names:
            loads[name].wait()
            waited.add(name)

    first_sem = {}

    def load_wide(name, src, dst):
        first_sem[name] = len(loads)
        for c in range(ROWS // RC):
            rows = pl.ds(c * RC, RC)
            load(f"{name}{c}", src.at[rows, :], dst.at[rows, :])

    def over_chunks(name, src, dst, body):
        waited.update(f"{name}{c}" for c in range(ROWS // RC))

        @pl.loop(0, ROWS // RC)
        def _(c):
            rows = pl.ds(pl.multiple_of(c * RC, RC), RC)
            pltpu.make_async_copy(
                src.at[rows, :], dst.at[rows, :], load_sem.at[first_sem[name] + c]
            ).wait()
            body(c, rows)

    load("len", lengths, len_ref)
    load("hes", hes.at[:, 0], hes_v)
    load("qry", qry, qry_v)
    load("wnar", wnar, wnar_v)
    load("gk", gk, gk_v)
    load("gv", gv, gv_v)
    for m in range(3):
        load(f"win{m}", win.at[m], win_v.at[pl.ds(m * PR, PR)])
    load_wide("xa", xa, xa_v)
    load("wq", wwide.at[0], wwide_v.at[0])
    load_wide("gq", gq, gq_v)
    load("win3", win.at[3], win_v.at[pl.ds(4 * PR, PR)])
    load_wide("xc", xc, xc_v)
    load("wo", wwide.at[1], wwide_v.at[1])
    load_wide("go", go, go_v)

    barrier = pltpu.get_barrier_semaphore()

    @pl.loop(1, OWN)
    def _(s):
        to = ((fy + s // SIDE) % SIDE) * SIDE + (fx + s % SIDE) % SIDE
        pl.semaphore_signal(barrier, inc=1, device_id={"feat": to}, device_id_type=MESH)

    @pl.loop(1, EXN)
    def _(s):
        pl.semaphore_signal(barrier, inc=1, device_id={"ex": (ex + s) % EXN}, device_id_type=MESH)

    def halves(x):
        high = x.astype(BF)
        return high, (x - high.astype(F32)).astype(BF)

    ready("hes", "qry")

    @pl.loop(0, 4)
    def _(m):
        q_high, q_low = halves(qry_v[:, m, :])
        h_high, h_low = halves(hes_v[m])
        hb_v[m] = h_high
        both = jnp.dot(
            jnp.concatenate([q_high, q_low], axis=0), h_high, preferred_element_type=F32
        )
        rest = jnp.dot(q_high, h_low, preferred_element_type=F32)
        ploc[m] = (both[0:QL] + (both[QL:2 * QL] + rest)).astype(BF)

    pl.semaphore_wait(barrier, OWN - 1 + EXN - 1)

    my_q = pl.ds(pl.multiple_of(ex * QL, QL), QL)

    @pl.loop(1, EXN)
    def _(s):
        pltpu.make_async_remote_copy(
            src_ref=ploc, dst_ref=pall.at[:, my_q, :], send_sem=p_send, recv_sem=p_recv,
            device_id={"ex": (ex + s) % EXN}, device_id_type=MESH,
        ).start()
    pall[:, my_q, :] = ploc[...]

    half = lax.broadcasted_iota(jnp.int32, (128, 128), 1) < PR

    def rows_of(k):
        return pl.ds(pl.multiple_of(k * EXD, EXD), EXD)

    def project(m, target_v, weight, c, rows):
        o_t = lax.dot_general(
            weight[...], target_v[rows, :], NT, preferred_element_type=F32
        )
        count = o_t.shape[1] // 128
        for b in range(count):
            ot[m, c * count + b] = o_t[:, b * 128:(b + 1) * 128]

    def split(x, left, twice):
        turned = x if twice else pltpu.roll(x, PR, axis=1)
        on_left, on_right = (x, turned) if left else (turned, x)
        return jnp.where(half, on_left, 0.0).astype(BF), jnp.where(half, 0.0, on_right).astype(BF)

    def pair(m, g):
        rows = pl.ds(g * 128, 128)
        if m == QUERY:
            return split(pin[rows, 0:128], True, False)
        if m == KEY:
            return split(pin[rows, 0:128], False, False)
        if m == VALUE:
            return split(pin[rows, 128:256], True, True)
        return split(pin_o[rows, :], True, True)

    def outer(m, g):
        parts = [
            [ot[m, g, pl.ds(2 * ih + il, 16, stride=4), :].astype(BF) for il in range(2)]
            for ih in range(2)
        ]
        lhs = jnp.concatenate([jnp.concatenate(p, axis=1) for p in parts], axis=0)
        blocks = []
        for e in range(4):
            mk = mask_v[4 * g + e]
            blocks.append(lhs * jnp.concatenate([mk, mk], axis=0))
        lhs = jnp.concatenate(blocks, axis=0)
        rhs = jnp.concatenate(pair(m, g), axis=0)
        r = jnp.dot(lhs, rhs, preferred_element_type=F32)
        for e in range(4):
            for ih in range(2):
                at = (2 * e + ih) * 16
                g32[m, ih, pl.ds(4 * g + e, 16, stride=PITCH), :] = r[at:at + 16, :]

    def gather(m):
        for k in range(OWN):
            gsend[m, k * EXD:(k + 1) * EXD, :] = jnp.concatenate(
                [g32[m, ih, k * PITCH:k * PITCH + EXD, :] for ih in range(2)], axis=1
            ).astype(BF)

    def send(m):
        for i in FAR_FIRST:
            to = ahead(i)
            pltpu.make_async_remote_copy(
                src_ref=gsend.at[m, rows_of(to), :],
                dst_ref=grec.at[m, pl.ds(i * EXD, EXD), :],
                send_sem=g_send, recv_sem=g_recv.at[m if m < OUTPUT else OUTPUT + GROUP_OF[i]],
                device_id={"feat": to}, device_id_type=MESH,
            ).start()
        grec[m, 0:EXD, :] = gsend[m, rows_of(ft), :]

    def project_in(dst, source_v, weight, rows):
        dst[rows, :] = lax.dot_general(
            source_v[rows, :], weight[...], NT, preferred_element_type=F32
        )

    every = pl.ds(0, ROWS)
    ready("len")
    lane = lax.broadcasted_iota(jnp.int32, (16, 256), 1)
    lane_e = (lane // LEN) % 4
    lane_t = lane % LEN

    @pl.loop(0, EXD)
    def _(e):
        on = (lane_e == e % 4) & (lane_t < len_ref[e])
        mask_v[e] = jnp.where(on, 1.0, 0.0).astype(BF)

    ready("wnar", "gk", "gv")
    project(KEY, gk_v, wnar_v.at[0], 0, every)
    project(VALUE, gv_v, wnar_v.at[1], 0, every)
    ready("win0", "win1", "win2")
    win_v[3 * PR:4 * PR, :] = win_v[2 * PR:3 * PR, :]
    over_chunks("xa", xa, xa_v, lambda c, rows: project_in(pin, xa_v, win_v.at[0:4 * PR], rows))
    for m in (KEY, VALUE):
        for g in range(EXD // 4):
            outer(m, g)
        gather(m)
        send(m)
    ready("wq")
    over_chunks("gq", gq, gq_v, lambda c, rows: project(QUERY, gq_v, wwide_v.at[0], c, rows))
    for g in range(EXD // 4):
        outer(QUERY, g)
    gather(QUERY)
    send(QUERY)
    ready("win3")
    win_v[5 * PR:6 * PR, :] = win_v[4 * PR:5 * PR, :]
    over_chunks("xc", xc, xc_v, lambda c, rows: project_in(pin_o, xc_v, win_v.at[4 * PR:6 * PR], rows))
    ready("wo")
    over_chunks("go", go, go_v, lambda c, rows: project(OUTPUT, go_v, wwide_v.at[1], c, rows))
    for g in range(EXD // 4):
        outer(OUTPUT, g)
    gather(OUTPUT)
    send(OUTPUT)

    others = (OWN - 1) * EXD

    def products(m, rows):
        got = grec[m, rows, :]
        raw = lax.dot_general(got, pall[m], NT, preferred_element_type=F32)
        own = jnp.dot(got, hb_v[m], preferred_element_type=F32) * got.astype(F32)
        return raw, own[:, 0:128] + own[:, 128:256]

    arrived(pall.at[:, pl.ds(0, QN - QL), :], p_recv)
    for m in (KEY, VALUE, QUERY):
        arrived(grec.at[m, pl.ds(0, others), :], g_recv.at[m])
        raw, own = products(m, slice(0, OWN * EXD))
        if m == KEY:
            acc[...] = raw
            tacc[...] = own
        else:
            acc[...] += raw
            tacc[...] += own

    for n, group in enumerate(GROUPS):
        partners = [i for i in group if i > 0]
        arrived(grec.at[OUTPUT, pl.ds(0, len(partners) * EXD), :], g_recv.at[OUTPUT + n])
        rows = slice(group[0] * EXD, (group[-1] + 1) * EXD)
        raw, own = products(OUTPUT, rows)
        raw = raw + acc[rows, :]
        own = own + tacc[rows, :]
        own = own + pltpu.roll(own, 64, axis=1)
        high = own.astype(BF).astype(F32)
        left = lax.broadcasted_iota(jnp.int32, own.shape, 1) < 64
        sbuf[rows, 0:QN] = raw.astype(BF)
        sbuf[rows, QN:W] = jnp.where(left, high, own - high).astype(BF)
        for i in partners:
            at = pl.ds(i * EXD, EXD)
            pltpu.make_async_remote_copy(
                src_ref=sbuf.at[at, :], dst_ref=srec.at[at, :], send_sem=s_send,
                recv_sem=s_recv.at[n], device_id={"feat": behind(i)}, device_id_type=MESH,
            ).start()

    total = sbuf[0:EXD, :].astype(F32)
    for n, group in enumerate(GROUPS):
        partners = [i for i in group if i > 0]
        arrived(srec.at[pl.ds(0, len(partners) * EXD), :], s_recv.at[n])
        for i in partners:
            total = total + srec[i * EXD:(i + 1) * EXD, :].astype(F32)
    self_inf = jnp.sum(total[:, QN:W], axis=1, keepdims=True)
    out_ref[...] = total[:, 0:QN] * lax.rsqrt(self_inf + 1e-06)

    arrived(gsend.at[:, pl.ds(0, others), :], g_send)
    arrived(sbuf.at[pl.ds(0, others), :], s_send)
    arrived(pall.at[:, pl.ds(0, QN - QL), :], p_send)


def per_device(
    lengths, attn_in, context, grad_q, grad_k, grad_v, grad_o,
    proj_in, proj_out_wide, proj_out_narrow, inv_hessian, query_feats,
):
    def flat(x):
        return x.reshape(ROWS, x.shape[-1])

    any_space = pl.BlockSpec(memory_space=pl.ANY)
    dma = pltpu.SemaphoreType.DMA
    return pl.pallas_call(
        kernel,
        out_shape=jax.ShapeDtypeStruct((EXD, QN), F32),
        in_specs=[any_space] * 12,
        out_specs=pl.BlockSpec(memory_space=pltpu.VMEM),
        scratch_shapes=[
            pltpu.SMEM((EXD,), jnp.int32),
            pltpu.VMEM((ROWS, D), BF),
            pltpu.VMEM((ROWS, D), BF),
            pltpu.VMEM((ROWS, D), BF),
            pltpu.VMEM((ROWS, KVW), BF),
            pltpu.VMEM((ROWS, KVW), BF),
            pltpu.VMEM((ROWS, D), BF),
            pltpu.VMEM((6 * PR, D), BF),
            pltpu.VMEM((2, PR, D), BF),
            pltpu.VMEM((2, PR, KVW), BF),
            pltpu.VMEM((4, HB, HB), F32),
            pltpu.VMEM((QL, 4, HB), F32),
            pltpu.VMEM((4, HB, HB), BF),
            pltpu.VMEM((4, QL, HB), BF),
            pltpu.VMEM((4, QN, HB), BF),
            pltpu.VMEM((ROWS, 256), F32),
            pltpu.VMEM((ROWS, 128), F32),
            pltpu.VMEM((4, EXD // 4, PR, 128), F32),
            pltpu.VMEM((EXD, 16, 256), BF),
            pltpu.VMEM((4, 2, OWN * PITCH, 128), F32),
            pltpu.VMEM((4, OWN * EXD, HB), BF),
            pltpu.VMEM((4, OWN * EXD, HB), BF),
            pltpu.VMEM((OWN * EXD, QN), F32),
            pltpu.VMEM((OWN * EXD, 128), F32),
            pltpu.VMEM((OWN * EXD, W), BF),
            pltpu.VMEM((OWN * EXD, W), BF),
            dma((20,)),
            dma,
            dma,
            dma,
            dma((OUTPUT + len(GROUPS),)),
            dma,
            dma((len(GROUPS),)),
        ],
        compiler_params=pltpu.CompilerParams(
            collective_id=0, has_side_effects=True, vmem_limit_bytes=56 << 20
        ),
    )(
        lengths, flat(attn_in), flat(context), flat(grad_q), flat(grad_k), flat(grad_v),
        flat(grad_o), proj_in, proj_out_wide, proj_out_narrow, inv_hessian, query_feats,
    )


def solution(mesh):
    both = P(("ex", "feat"), None, None)
    in_specs = (
        P(("ex", "feat")), both, both, both, both, both, both,
        P(), P(), P(),
        P(None, "feat", None, None),
        P("ex", None, "feat"),
    )
    return jax.shard_map(
        per_device, mesh=mesh, in_specs=in_specs, out_specs=P(("ex", "feat"), None), check_vma=False
    )
```

```python
import jax
import jax.numpy as jnp
from jax import lax
from jax.experimental import pallas as pl
from jax.experimental.pallas import tpu as pltpu
from jax.sharding import PartitionSpec as P

MESH = pl.DeviceIdType.MESH
NT = (((1,), (1,)), ((), ()))
BF = jnp.bfloat16
F32 = jnp.float32

D = 4096
KVW = 1024
PR = 64
HB = 256
LEN = 32
EXD = 16
ROWS = EXD * LEN
SIDE = 4
OWN = SIDE * SIDE
EXN = 8
QL = 32
QN = 256
W = 384
RC = 256
PITCH = 17
QUERY, KEY, VALUE, OUTPUT = range(4)


def hops(s):
    dy, dx = divmod(s, SIDE)
    return min(dy, SIDE - dy) + min(dx, SIDE - dx)


SLOTS = sorted(range(OWN), key=hops)
GROUPS = [[i for i in range(OWN) if max(hops(SLOTS[i]), 1) == h] for h in range(1, SIDE + 1)]
GROUP_OF = {i: n for n, g in enumerate(GROUPS) for i in g}
FAR_FIRST = range(OWN - 1, 0, -1)


def arrived(ref, sem):
    pltpu.make_async_copy(ref, ref, sem).wait()


def kernel(
    lengths, xa, xc, gq, gk, gv, go, win, wwide, wnar, hes, qry, out_ref,
    len_ref, xa_v, xc_v, gq_v, gk_v, gv_v, go_v, win_v, wwide_v, wnar_v, hes_v, qry_v,
    hb_v, ploc, pall, pin, pin_o, ot, mask_v, g32, gsend, grec, acc, tacc, sbuf, srec,
    load_sem, p_send, p_recv, g_send, g_recv, s_send, s_recv,
):
    ex = lax.axis_index("ex")
    ft = lax.axis_index("feat")
    xs = [(ft % SIDE + d) % SIDE for d in range(SIDE)]
    ys = [((ft // SIDE + d) % SIDE) * SIDE for d in range(SIDE)]

    def ahead(i):
        dy, dx = divmod(SLOTS[i], SIDE)
        return ys[dy] + xs[dx]

    def behind(i):
        dy, dx = divmod(SLOTS[i], SIDE)
        return ys[-dy % SIDE] + xs[-dx % SIDE]

    loads = {}
    waited = set()

    def load(name, src, dst):
        copy = pltpu.make_async_copy(src, dst, load_sem.at[len(loads)])
        copy.start()
        loads[name] = copy

    def ready(*names):
        for name in names:
            loads[name].wait()
            waited.add(name)

    first_sem = {}

    def load_wide(name, src, dst):
        first_sem[name] = len(loads)
        for c in range(ROWS // RC):
            rows = pl.ds(c * RC, RC)
            load(f"{name}{c}", src.at[rows, :], dst.at[rows, :])

    def all_rows_of(name, body):
        ready(f"{name}0", f"{name}1")
        body(0, pl.ds(0, ROWS))

    def over_chunks(name, src, dst, body):
        waited.update(f"{name}{c}" for c in range(ROWS // RC))

        @pl.loop(0, ROWS // RC)
        def _(c):
            rows = pl.ds(pl.multiple_of(c * RC, RC), RC)
            pltpu.make_async_copy(
                src.at[rows, :], dst.at[rows, :], load_sem.at[first_sem[name] + c]
            ).wait()
            body(c, rows)

    load("len", lengths, len_ref)
    load("hes", hes.at[:, 0], hes_v)
    load("qry", qry, qry_v)
    load("wnar", wnar, wnar_v)
    load("gk", gk, gk_v)
    load("gv", gv, gv_v)
    for m in range(3):
        load(f"win{m}", win.at[m], win_v.at[pl.ds(m * PR, PR)])
    load_wide("xa", xa, xa_v)
    load("wq", wwide.at[0], wwide_v.at[0])
    load_wide("gq", gq, gq_v)
    load("win3", win.at[3], win_v.at[pl.ds(4 * PR, PR)])
    load_wide("xc", xc, xc_v)
    load("wo", wwide.at[1], wwide_v.at[1])
    load_wide("go", go, go_v)

    barrier = pltpu.get_barrier_semaphore()

    for d in range(1, EXN):
        pl.semaphore_signal(barrier, inc=1, device_id={"ex": (ex + d) % EXN}, device_id_type=MESH)
    for i in FAR_FIRST:
        pl.semaphore_signal(barrier, inc=1, device_id={"feat": ahead(i)}, device_id_type=MESH)

    def halves(x):
        high = x.astype(BF)
        return high, (x - high.astype(F32)).astype(BF)

    ready("hes", "qry")

    @pl.loop(0, 4)
    def _(m):
        q_high, q_low = halves(qry_v[:, m, :])
        h_high, h_low = halves(hes_v[m])
        hb_v[m] = h_high
        both = jnp.dot(
            jnp.concatenate([q_high, q_low], axis=0), h_high, preferred_element_type=F32
        )
        rest = jnp.dot(q_high, h_low, preferred_element_type=F32)
        ploc[m] = (both[0:QL] + (both[QL:2 * QL] + rest)).astype(BF)

    my_q = pl.ds(pl.multiple_of(ex * QL, QL), QL)

    def enter():
        pl.semaphore_wait(barrier, OWN - 1 + EXN - 1)

        @pl.loop(1, EXN)
        def _(s):
            pltpu.make_async_remote_copy(
                src_ref=ploc, dst_ref=pall.at[:, my_q, :], send_sem=p_send, recv_sem=p_recv,
                device_id={"ex": (ex + s) % EXN},
                device_id_type=MESH,
            ).start()

    late = ex >= EXN // 2
    pall[:, my_q, :] = ploc[...]

    half = lax.broadcasted_iota(jnp.int32, (128, 128), 1) < PR

    def rows_of(k):
        return pl.ds(pl.multiple_of(k * EXD, EXD), EXD)

    def project(m, target_v, weight, c, rows):
        o_t = lax.dot_general(
            weight[...], target_v[rows, :], NT, preferred_element_type=F32
        )
        count = o_t.shape[1] // 128
        for b in range(count):
            ot[m, c * count + b] = o_t[:, b * 128:(b + 1) * 128]

    def split(x, left, twice):
        turned = x if twice else pltpu.roll(x, PR, axis=1)
        on_left, on_right = (x, turned) if left else (turned, x)
        return jnp.where(half, on_left, 0.0).astype(BF), jnp.where(half, 0.0, on_right).astype(BF)

    def pair(m, g):
        rows = pl.ds(g * 128, 128)
        if m == QUERY:
            return split(pin[rows, 0:128], True, False)
        if m == KEY:
            return split(pin[rows, 0:128], False, False)
        if m == VALUE:
            return split(pin[rows, 128:256], True, True)
        return split(pin_o[rows, :], True, True)

    def outer(m, g):
        parts = [
            [ot[m, g, pl.ds(2 * ih + il, 16, stride=4), :].astype(BF) for il in range(2)]
            for ih in range(2)
        ]
        lhs = jnp.concatenate([jnp.concatenate(p, axis=1) for p in parts], axis=0)
        blocks = []
        for e in range(4):
            mk = mask_v[4 * g + e]
            blocks.append(lhs * jnp.concatenate([mk, mk], axis=0))
        lhs = jnp.concatenate(blocks, axis=0)
        rhs = jnp.concatenate(pair(m, g), axis=0)
        r = jnp.dot(lhs, rhs, preferred_element_type=F32)
        for e in range(4):
            for ih in range(2):
                at = (2 * e + ih) * 16
                g32[m, ih, pl.ds(4 * g + e, 16, stride=PITCH), :] = r[at:at + 16, :]

    def gather(m):
        for k in range(OWN):
            gsend[m, k * EXD:(k + 1) * EXD, :] = jnp.concatenate(
                [g32[m, ih, k * PITCH:k * PITCH + EXD, :] for ih in range(2)], axis=1
            ).astype(BF)

    def send(m):
        for i in FAR_FIRST:
            to = ahead(i)
            pltpu.make_async_remote_copy(
                src_ref=gsend.at[m, rows_of(to), :],
                dst_ref=grec.at[m, pl.ds(i * EXD, EXD), :],
                send_sem=g_send, recv_sem=g_recv.at[m if m < OUTPUT else OUTPUT + GROUP_OF[i]],
                device_id={"feat": to}, device_id_type=MESH,
            ).start()
        grec[m, 0:EXD, :] = gsend[m, rows_of(ft), :]

    def project_in(dst, source_v, weight, rows):
        dst[rows, :] = lax.dot_general(
            source_v[rows, :], weight[...], NT, preferred_element_type=F32
        )

    every = pl.ds(0, ROWS)
    ready("len")
    lane = lax.broadcasted_iota(jnp.int32, (16, 256), 1)
    lane_e = (lane // LEN) % 4
    lane_t = lane % LEN

    @pl.loop(0, EXD)
    def _(e):
        on = (lane_e == e % 4) & (lane_t < len_ref[e])
        mask_v[e] = jnp.where(on, 1.0, 0.0).astype(BF)

    ready("wnar", "gk", "gv")
    project(KEY, gk_v, wnar_v.at[0], 0, every)
    project(VALUE, gv_v, wnar_v.at[1], 0, every)
    pl.when(late)(enter)
    ready("win0", "win1", "win2")
    win_v[3 * PR:4 * PR, :] = win_v[2 * PR:3 * PR, :]
    over_chunks("xa", xa, xa_v, lambda c, rows: project_in(pin, xa_v, win_v.at[0:4 * PR], rows))
    pl.when(jnp.logical_not(late))(enter)
    for m in (KEY, VALUE):
        for g in range(EXD // 4):
            outer(m, g)
        gather(m)
        send(m)
    ready("wq")
    all_rows_of("gq", lambda c, rows: project(QUERY, gq_v, wwide_v.at[0], c, rows))
    for g in range(EXD // 4):
        outer(QUERY, g)
    gather(QUERY)
    send(QUERY)
    ready("win3")
    win_v[5 * PR:6 * PR, :] = win_v[4 * PR:5 * PR, :]
    all_rows_of("xc", lambda c, rows: project_in(pin_o, xc_v, win_v.at[4 * PR:6 * PR], rows))
    ready("wo")
    over_chunks("go", go, go_v, lambda c, rows: project(OUTPUT, go_v, wwide_v.at[1], c, rows))
    for g in range(EXD // 4):
        outer(OUTPUT, g)
    gather(OUTPUT)
    send(OUTPUT)

    others = (OWN - 1) * EXD

    def raw_part(m, rows):
        return lax.dot_general(grec[m, rows, :], pall[m], NT, preferred_element_type=F32)

    def self_part(m, rows):
        got = grec[m, rows, :]
        own = jnp.dot(got, hb_v[m], preferred_element_type=F32) * got.astype(F32)
        return own[:, 0:128] + own[:, 128:256]

    early = (KEY, VALUE, QUERY)
    all_rows = slice(0, OWN * EXD)
    for m in early:
        arrived(grec.at[m, pl.ds(0, others), :], g_recv.at[m])
        own = self_part(m, all_rows)
        tacc[...] = own if m == KEY else tacc[...] + own
    arrived(pall.at[:, pl.ds(0, QN - QL), :], p_recv)
    for m in early:
        raw = raw_part(m, all_rows)
        acc[...] = raw if m == KEY else acc[...] + raw

    for n, group in enumerate(GROUPS):
        partners = [i for i in group if i > 0]
        arrived(grec.at[OUTPUT, pl.ds(0, len(partners) * EXD), :], g_recv.at[OUTPUT + n])
        rows = slice(group[0] * EXD, (group[-1] + 1) * EXD)
        raw = raw_part(OUTPUT, rows) + acc[rows, :]
        own = self_part(OUTPUT, rows) + tacc[rows, :]
        own = own + pltpu.roll(own, 64, axis=1)
        high = own.astype(BF).astype(F32)
        left = lax.broadcasted_iota(jnp.int32, own.shape, 1) < 64
        sbuf[rows, 0:QN] = raw.astype(BF)
        sbuf[rows, QN:W] = jnp.where(left, high, own - high).astype(BF)
        for i in partners:
            at = pl.ds(i * EXD, EXD)
            pltpu.make_async_remote_copy(
                src_ref=sbuf.at[at, :], dst_ref=srec.at[at, :], send_sem=s_send,
                recv_sem=s_recv.at[n], device_id={"feat": behind(i)}, device_id_type=MESH,
            ).start()

    total = sbuf[0:EXD, :].astype(F32)
    for n, group in enumerate(GROUPS):
        partners = [i for i in group if i > 0]
        arrived(srec.at[pl.ds(0, len(partners) * EXD), :], s_recv.at[n])
        for i in partners:
            total = total + srec[i * EXD:(i + 1) * EXD, :].astype(F32)
    self_inf = jnp.sum(total[:, QN:W], axis=1, keepdims=True)
    out_ref[...] = total[:, 0:QN] * lax.rsqrt(self_inf + 1e-06)

    arrived(gsend.at[:, pl.ds(0, others), :], g_send)
    arrived(sbuf.at[pl.ds(0, others), :], s_send)
    arrived(pall.at[:, pl.ds(0, QN - QL), :], p_send)


def per_device(
    lengths, attn_in, context, grad_q, grad_k, grad_v, grad_o,
    proj_in, proj_out_wide, proj_out_narrow, inv_hessian, query_feats,
):
    def flat(x):
        return x.reshape(ROWS, x.shape[-1])

    any_space = pl.BlockSpec(memory_space=pl.ANY)
    dma = pltpu.SemaphoreType.DMA
    return pl.pallas_call(
        kernel,
        out_shape=jax.ShapeDtypeStruct((EXD, QN), F32),
        in_specs=[any_space] * 12,
        out_specs=pl.BlockSpec(memory_space=pltpu.VMEM),
        scratch_shapes=[
            pltpu.SMEM((EXD,), jnp.int32),
            pltpu.VMEM((ROWS, D), BF),
            pltpu.VMEM((ROWS, D), BF),
            pltpu.VMEM((ROWS, D), BF),
            pltpu.VMEM((ROWS, KVW), BF),
            pltpu.VMEM((ROWS, KVW), BF),
            pltpu.VMEM((ROWS, D), BF),
            pltpu.VMEM((6 * PR, D), BF),
            pltpu.VMEM((2, PR, D), BF),
            pltpu.VMEM((2, PR, KVW), BF),
            pltpu.VMEM((4, HB, HB), F32),
            pltpu.VMEM((QL, 4, HB), F32),
            pltpu.VMEM((4, HB, HB), BF),
            pltpu.VMEM((4, QL, HB), BF),
            pltpu.VMEM((4, QN, HB), BF),
            pltpu.VMEM((ROWS, 256), F32),
            pltpu.VMEM((ROWS, 128), F32),
            pltpu.VMEM((4, EXD // 4, PR, 128), F32),
            pltpu.VMEM((EXD, 16, 256), BF),
            pltpu.VMEM((4, 2, OWN * PITCH, 128), F32),
            pltpu.VMEM((4, OWN * EXD, HB), BF),
            pltpu.VMEM((4, OWN * EXD, HB), BF),
            pltpu.VMEM((OWN * EXD, QN), F32),
            pltpu.VMEM((OWN * EXD, 128), F32),
            pltpu.VMEM((OWN * EXD, W), BF),
            pltpu.VMEM((OWN * EXD, W), BF),
            dma((20,)),
            dma,
            dma,
            dma,
            dma((OUTPUT + len(GROUPS),)),
            dma,
            dma((len(GROUPS),)),
        ],
        compiler_params=pltpu.CompilerParams(
            collective_id=0, has_side_effects=True, vmem_limit_bytes=56 << 20
        ),
    )(
        lengths, flat(attn_in), flat(context), flat(grad_q), flat(grad_k), flat(grad_v),
        flat(grad_o), proj_in, proj_out_wide, proj_out_narrow, inv_hessian, query_feats,
    )


def solution(mesh):
    both = P(("ex", "feat"), None, None)
    in_specs = (
        P(("ex", "feat")), both, both, both, both, both, both,
        P(), P(), P(),
        P(None, "feat", None, None),
        P("ex", None, "feat"),
    )
    return jax.shard_map(
        per_device, mesh=mesh, in_specs=in_specs, out_specs=P(("ex", "feat"), None), check_vma=False
    )
```

```python
import jax
import jax.numpy as jnp
from jax import lax
from jax.experimental import pallas as pl
from jax.experimental.pallas import tpu as pltpu
from jax.sharding import PartitionSpec as P

MESH = pl.DeviceIdType.MESH
NT = (((1,), (1,)), ((), ()))
BF = jnp.bfloat16
F32 = jnp.float32

D = 4096
KVW = 1024
PR = 64
HB = 256
LEN = 32
EXD = 16
ROWS = EXD * LEN
SIDE = 4
OWN = SIDE * SIDE
EXN = 8
QL = 32
QN = 256
W = 384
RC = 256
PITCH = 17
QUERY, KEY, VALUE, OUTPUT = range(4)


def hops(s):
    dy, dx = divmod(s, SIDE)
    return min(dy, SIDE - dy) + min(dx, SIDE - dx)


SLOTS = sorted(range(OWN), key=hops)
GROUPS = [[i for i in range(OWN) if max(hops(SLOTS[i]), 1) == h] for h in range(1, SIDE + 1)]
GROUP_OF = {i: n for n, g in enumerate(GROUPS) for i in g}
FAR_FIRST = range(OWN - 1, 0, -1)


def arrived(ref, sem):
    pltpu.make_async_copy(ref, ref, sem).wait()


def kernel(
    lengths, xa, xc, gq, gk, gv, go, win, wwide, wnar, hes, qry, out_ref,
    len_ref, xa_v, xc_v, gq_v, gk_v, gv_v, go_v, win_v, wwide_v, wnar_v, hes_v, qry_v,
    hb_v, ploc, pall, pin, pin_o, ot, mask_v, g32, gsend, grec, acc, tacc, sbuf, srec,
    load_sem, p_send, p_recv, g_send, g_recv, s_send, s_recv,
):
    ex = lax.axis_index("ex")
    ft = lax.axis_index("feat")
    xs = [(ft % SIDE + d) % SIDE for d in range(SIDE)]
    ys = [((ft // SIDE + d) % SIDE) * SIDE for d in range(SIDE)]

    def ahead(i):
        dy, dx = divmod(SLOTS[i], SIDE)
        return ys[dy] + xs[dx]

    def behind(i):
        dy, dx = divmod(SLOTS[i], SIDE)
        return ys[-dy % SIDE] + xs[-dx % SIDE]

    loads = {}
    waited = set()

    def load(name, src, dst):
        copy = pltpu.make_async_copy(src, dst, load_sem.at[len(loads)])
        copy.start()
        loads[name] = copy

    def ready(*names):
        for name in names:
            loads[name].wait()
            waited.add(name)

    first_sem = {}

    def load_wide(name, src, dst):
        first_sem[name] = len(loads)
        for c in range(ROWS // RC):
            rows = pl.ds(c * RC, RC)
            load(f"{name}{c}", src.at[rows, :], dst.at[rows, :])

    def all_rows_of(name, body):
        ready(f"{name}0", f"{name}1")
        body(0, pl.ds(0, ROWS))

    def over_chunks(name, src, dst, body):
        waited.update(f"{name}{c}" for c in range(ROWS // RC))

        @pl.loop(0, ROWS // RC)
        def _(c):
            rows = pl.ds(pl.multiple_of(c * RC, RC), RC)
            pltpu.make_async_copy(
                src.at[rows, :], dst.at[rows, :], load_sem.at[first_sem[name] + c]
            ).wait()
            body(c, rows)

    load("len", lengths, len_ref)
    load("hes", hes.at[:, 0], hes_v)
    load("qry", qry, qry_v)
    load("wnar", wnar, wnar_v)
    load("gk", gk, gk_v)
    load("gv", gv, gv_v)
    for m in range(3):
        load(f"win{m}", win.at[m], win_v.at[pl.ds(m * PR, PR)])
    load_wide("xa", xa, xa_v)
    load("wq", wwide.at[0], wwide_v.at[0])
    load_wide("gq", gq, gq_v)
    load("win3", win.at[3], win_v.at[pl.ds(4 * PR, PR)])
    load_wide("xc", xc, xc_v)
    load("wo", wwide.at[1], wwide_v.at[1])
    load_wide("go", go, go_v)

    barrier = pltpu.get_barrier_semaphore()

    for d in range(1, EXN):
        pl.semaphore_signal(barrier, inc=1, device_id={"ex": (ex + d) % EXN}, device_id_type=MESH)
    for i in FAR_FIRST:
        pl.semaphore_signal(barrier, inc=1, device_id={"feat": ahead(i)}, device_id_type=MESH)

    def halves(x):
        high = x.astype(BF)
        return high, (x - high.astype(F32)).astype(BF)

    ready("hes", "qry")

    @pl.loop(0, 4)
    def _(m):
        q_high, q_low = halves(qry_v[:, m, :])
        h_high, h_low = halves(hes_v[m])
        hb_v[m] = h_high
        both = jnp.dot(
            jnp.concatenate([q_high, q_low], axis=0), h_high, preferred_element_type=F32
        )
        rest = jnp.dot(q_high, h_low, preferred_element_type=F32)
        ploc[m] = (both[0:QL] + (both[QL:2 * QL] + rest)).astype(BF)

    my_q = pl.ds(pl.multiple_of(ex * QL, QL), QL)

    def enter():
        pl.semaphore_wait(barrier, OWN - 1 + EXN - 1)

        @pl.loop(0, EXN - 1)
        def _(s):
            to = jnp.where(s < ex, s, s + 1)
            pltpu.make_async_remote_copy(
                src_ref=ploc, dst_ref=pall.at[:, my_q, :], send_sem=p_send, recv_sem=p_recv,
                device_id={"ex": to},
                device_id_type=MESH,
            ).start()

    late = ex >= EXN // 2
    pall[:, my_q, :] = ploc[...]

    half = lax.broadcasted_iota(jnp.int32, (128, 128), 1) < PR

    def rows_of(k):
        return pl.ds(pl.multiple_of(k * EXD, EXD), EXD)

    def project(m, target_v, weight, c, rows):
        o_t = lax.dot_general(
            weight[...], target_v[rows, :], NT, preferred_element_type=F32
        )
        count = o_t.shape[1] // 128
        for b in range(count):
            ot[m, c * count + b] = o_t[:, b * 128:(b + 1) * 128]

    def split(x, left, twice):
        turned = x if twice else pltpu.roll(x, PR, axis=1)
        on_left, on_right = (x, turned) if left else (turned, x)
        return jnp.where(half, on_left, 0.0).astype(BF), jnp.where(half, 0.0, on_right).astype(BF)

    def pair(m, g):
        rows = pl.ds(g * 128, 128)
        if m == QUERY:
            return split(pin[rows, 0:128], True, False)
        if m == KEY:
            return split(pin[rows, 0:128], False, False)
        if m == VALUE:
            return split(pin[rows, 128:256], True, True)
        return split(pin_o[rows, :], True, True)

    def outer(m, g):
        parts = [
            [ot[m, g, pl.ds(2 * ih + il, 16, stride=4), :].astype(BF) for il in range(2)]
            for ih in range(2)
        ]
        lhs = jnp.concatenate([jnp.concatenate(p, axis=1) for p in parts], axis=0)
        blocks = []
        for e in range(4):
            mk = mask_v[4 * g + e]
            blocks.append(lhs * jnp.concatenate([mk, mk], axis=0))
        lhs = jnp.concatenate(blocks, axis=0)
        rhs = jnp.concatenate(pair(m, g), axis=0)
        r = jnp.dot(lhs, rhs, preferred_element_type=F32)
        for e in range(4):
            for ih in range(2):
                at = (2 * e + ih) * 16
                g32[m, ih, pl.ds(4 * g + e, 16, stride=PITCH), :] = r[at:at + 16, :]

    def gather(m):
        for k in range(OWN):
            gsend[m, k * EXD:(k + 1) * EXD, :] = jnp.concatenate(
                [g32[m, ih, k * PITCH:k * PITCH + EXD, :] for ih in range(2)], axis=1
            ).astype(BF)

    def send(m):
        for i in FAR_FIRST:
            to = ahead(i)
            pltpu.make_async_remote_copy(
                src_ref=gsend.at[m, rows_of(to), :],
                dst_ref=grec.at[m, pl.ds(i * EXD, EXD), :],
                send_sem=g_send, recv_sem=g_recv.at[m if m < OUTPUT else OUTPUT + GROUP_OF[i]],
                device_id={"feat": to}, device_id_type=MESH,
            ).start()
        grec[m, 0:EXD, :] = gsend[m, rows_of(ft), :]

    def project_in(dst, source_v, weight, rows):
        dst[rows, :] = lax.dot_general(
            source_v[rows, :], weight[...], NT, preferred_element_type=F32
        )

    every = pl.ds(0, ROWS)
    ready("len")
    lane = lax.broadcasted_iota(jnp.int32, (16, 256), 1)
    lane_e = (lane // LEN) % 4
    lane_t = lane % LEN

    @pl.loop(0, EXD)
    def _(e):
        on = (lane_e == e % 4) & (lane_t < len_ref[e])
        mask_v[e] = jnp.where(on, 1.0, 0.0).astype(BF)

    ready("wnar", "gk", "gv")
    project(KEY, gk_v, wnar_v.at[0], 0, every)
    project(VALUE, gv_v, wnar_v.at[1], 0, every)
    pl.when(late)(enter)
    ready("win0", "win1", "win2")
    win_v[3 * PR:4 * PR, :] = win_v[2 * PR:3 * PR, :]
    over_chunks("xa", xa, xa_v, lambda c, rows: project_in(pin, xa_v, win_v.at[0:4 * PR], rows))
    pl.when(jnp.logical_not(late))(enter)
    for m in (KEY, VALUE):
        for g in range(EXD // 4):
            outer(m, g)
        gather(m)
        send(m)
    ready("wq")
    all_rows_of("gq", lambda c, rows: project(QUERY, gq_v, wwide_v.at[0], c, rows))
    for g in range(EXD // 4):
        outer(QUERY, g)
    gather(QUERY)
    send(QUERY)
    ready("win3")
    win_v[5 * PR:6 * PR, :] = win_v[4 * PR:5 * PR, :]
    all_rows_of("xc", lambda c, rows: project_in(pin_o, xc_v, win_v.at[4 * PR:6 * PR], rows))
    ready("wo")
    over_chunks("go", go, go_v, lambda c, rows: project(OUTPUT, go_v, wwide_v.at[1], c, rows))
    for g in range(EXD // 4):
        outer(OUTPUT, g)
    gather(OUTPUT)
    send(OUTPUT)

    others = (OWN - 1) * EXD

    def raw_part(m, rows):
        return lax.dot_general(grec[m, rows, :], pall[m], NT, preferred_element_type=F32)

    def self_part(m, rows):
        got = grec[m, rows, :]
        own = jnp.dot(got, hb_v[m], preferred_element_type=F32) * got.astype(F32)
        return own[:, 0:128] + own[:, 128:256]

    early = (KEY, VALUE, QUERY)
    all_rows = slice(0, OWN * EXD)
    for m in early:
        arrived(grec.at[m, pl.ds(0, others), :], g_recv.at[m])
        own = self_part(m, all_rows)
        tacc[...] = own if m == KEY else tacc[...] + own
    arrived(pall.at[:, pl.ds(0, QN - QL), :], p_recv)
    for m in early:
        raw = raw_part(m, all_rows)
        acc[...] = raw if m == KEY else acc[...] + raw

    for n, group in enumerate(GROUPS):
        partners = [i for i in group if i > 0]
        arrived(grec.at[OUTPUT, pl.ds(0, len(partners) * EXD), :], g_recv.at[OUTPUT + n])
        rows = slice(group[0] * EXD, (group[-1] + 1) * EXD)
        raw = raw_part(OUTPUT, rows) + acc[rows, :]
        own = self_part(OUTPUT, rows) + tacc[rows, :]
        own = own + pltpu.roll(own, 64, axis=1)
        high = own.astype(BF).astype(F32)
        left = lax.broadcasted_iota(jnp.int32, own.shape, 1) < 64
        sbuf[rows, 0:QN] = raw.astype(BF)
        sbuf[rows, QN:W] = jnp.where(left, high, own - high).astype(BF)
    for i in FAR_FIRST:
        at = pl.ds(i * EXD, EXD)
        pltpu.make_async_remote_copy(
            src_ref=sbuf.at[at, :], dst_ref=srec.at[at, :], send_sem=s_send,
            recv_sem=s_recv.at[GROUP_OF[i]], device_id={"feat": behind(i)}, device_id_type=MESH,
        ).start()

    total = sbuf[0:EXD, :].astype(F32)
    for n, group in enumerate(GROUPS):
        partners = [i for i in group if i > 0]
        arrived(srec.at[pl.ds(0, len(partners) * EXD), :], s_recv.at[n])
        for i in partners:
            total = total + srec[i * EXD:(i + 1) * EXD, :].astype(F32)
    self_inf = jnp.sum(total[:, QN:W], axis=1, keepdims=True)
    out_ref[...] = total[:, 0:QN] * lax.rsqrt(self_inf + 1e-06)

    arrived(gsend.at[:, pl.ds(0, others), :], g_send)
    arrived(sbuf.at[pl.ds(0, others), :], s_send)
    arrived(pall.at[:, pl.ds(0, QN - QL), :], p_send)


def per_device(
    lengths, attn_in, context, grad_q, grad_k, grad_v, grad_o,
    proj_in, proj_out_wide, proj_out_narrow, inv_hessian, query_feats,
):
    def flat(x):
        return x.reshape(ROWS, x.shape[-1])

    any_space = pl.BlockSpec(memory_space=pl.ANY)
    dma = pltpu.SemaphoreType.DMA
    return pl.pallas_call(
        kernel,
        out_shape=pltpu.VMEM((EXD, QN), F32),
        in_specs=[any_space] * 12,
        out_specs=pl.BlockSpec(memory_space=pltpu.VMEM),
        scratch_shapes=[
            pltpu.SMEM((EXD,), jnp.int32),
            pltpu.VMEM((ROWS, D), BF),
            pltpu.VMEM((ROWS, D), BF),
            pltpu.VMEM((ROWS, D), BF),
            pltpu.VMEM((ROWS, KVW), BF),
            pltpu.VMEM((ROWS, KVW), BF),
            pltpu.VMEM((ROWS, D), BF),
            pltpu.VMEM((6 * PR, D), BF),
            pltpu.VMEM((2, PR, D), BF),
            pltpu.VMEM((2, PR, KVW), BF),
            pltpu.VMEM((4, HB, HB), F32),
            pltpu.VMEM((QL, 4, HB), F32),
            pltpu.VMEM((4, HB, HB), BF),
            pltpu.VMEM((4, QL, HB), BF),
            pltpu.VMEM((4, QN, HB), BF),
            pltpu.VMEM((ROWS, 256), F32),
            pltpu.VMEM((ROWS, 128), F32),
            pltpu.VMEM((4, EXD // 4, PR, 128), F32),
            pltpu.VMEM((EXD, 16, 256), BF),
            pltpu.VMEM((4, 2, OWN * PITCH, 128), F32),
            pltpu.VMEM((4, OWN * EXD, HB), BF),
            pltpu.VMEM((4, OWN * EXD, HB), BF),
            pltpu.VMEM((OWN * EXD, QN), F32),
            pltpu.VMEM((OWN * EXD, 128), F32),
            pltpu.VMEM((OWN * EXD, W), BF),
            pltpu.VMEM((OWN * EXD, W), BF),
            dma((20,)),
            dma,
            dma,
            dma,
            dma((OUTPUT + len(GROUPS),)),
            dma,
            dma((len(GROUPS),)),
        ],
        compiler_params=pltpu.CompilerParams(
            collective_id=0, has_side_effects=True, vmem_limit_bytes=56 << 20
        ),
    )(
        lengths, flat(attn_in), flat(context), flat(grad_q), flat(grad_k), flat(grad_v),
        flat(grad_o), proj_in, proj_out_wide, proj_out_narrow, inv_hessian, query_feats,
    )


def solution(mesh):
    both = P(("ex", "feat"), None, None)
    in_specs = (
        P(("ex", "feat")), both, both, both, both, both, both,
        P(), P(), P(),
        P(None, "feat", None, None),
        P("ex", None, "feat"),
    )
    return jax.shard_map(
        per_device, mesh=mesh, in_specs=in_specs, out_specs=P(("ex", "feat"), None), check_vma=False
    )
```

```python
import jax
import jax.numpy as jnp
from jax import lax
from jax.experimental import pallas as pl
from jax.experimental.pallas import tpu as pltpu
from jax.sharding import PartitionSpec as P

MESH = pl.DeviceIdType.MESH
NT = (((1,), (1,)), ((), ()))
BF = jnp.bfloat16
F32 = jnp.float32

D = 4096
KVW = 1024
PR = 64
HB = 256
LEN = 32
EXD = 16
ROWS = EXD * LEN
SIDE = 4
OWN = SIDE * SIDE
EXN = 8
QL = 32
QN = 256
W = 384
RC = 256
PITCH = 17
QUERY, KEY, VALUE, OUTPUT = range(4)


def hops(s):
    dy, dx = divmod(s, SIDE)
    return min(dy, SIDE - dy) + min(dx, SIDE - dx)


SLOTS = sorted(range(OWN), key=hops)
GROUPS = [[i for i in range(OWN) if max(hops(SLOTS[i]), 1) == h] for h in range(1, SIDE + 1)]
GROUP_OF = {i: n for n, g in enumerate(GROUPS) for i in g}
FAR_FIRST = range(OWN - 1, 0, -1)


def arrived(ref, sem):
    pltpu.make_async_copy(ref, ref, sem).wait()


def kernel(
    lengths, xa, xc, gq, gk, gv, go, win, wwide, wnar, hes, qry, out_ref,
    len_ref, xa_v, xc_v, gq_v, gk_v, gv_v, go_v, win_v, wwide_v, wnar_v, hes_v, qry_v,
    hb_v, ploc, pall, pin, pin_o, ot, mask_v, g32, gsend, grec, acc, tacc, sbuf, srec,
    load_sem, p_send, p_recv, g_send, g_recv, s_send, s_recv,
):
    ex = lax.axis_index("ex")
    ft = lax.axis_index("feat")
    xs = [(ft % SIDE + d) % SIDE for d in range(SIDE)]
    ys = [((ft // SIDE + d) % SIDE) * SIDE for d in range(SIDE)]

    def ahead(i):
        dy, dx = divmod(SLOTS[i], SIDE)
        return ys[dy] + xs[dx]

    def behind(i):
        dy, dx = divmod(SLOTS[i], SIDE)
        return ys[-dy % SIDE] + xs[-dx % SIDE]

    loads = {}

    def load(name, src, dst):
        copy = pltpu.make_async_copy(src, dst, load_sem.at[len(loads)])
        copy.start()
        loads[name] = copy

    def ready(*names):
        for name in names:
            loads[name].wait()

    first_sem = {}

    def load_wide(name, src, dst):
        first_sem[name] = len(loads)
        for c in range(ROWS // RC):
            rows = pl.ds(c * RC, RC)
            load(f"{name}{c}", src.at[rows, :], dst.at[rows, :])

    def all_rows_of(name, body):
        ready(f"{name}0", f"{name}1")
        body(0, pl.ds(0, ROWS))

    def over_chunks(name, src, dst, body):
        @pl.loop(0, ROWS // RC)
        def _(c):
            rows = pl.ds(pl.multiple_of(c * RC, RC), RC)
            pltpu.make_async_copy(
                src.at[rows, :], dst.at[rows, :], load_sem.at[first_sem[name] + c]
            ).wait()
            body(c, rows)

    load("len", lengths, len_ref)
    load("hes", hes.at[:, 0], hes_v)
    load("qry", qry, qry_v)
    load("wnar", wnar, wnar_v)
    load("gk", gk, gk_v)
    load("gv", gv, gv_v)
    for m in range(3):
        load(f"win{m}", win.at[m], win_v.at[pl.ds(m * PR, PR)])
    load_wide("xa", xa, xa_v)
    load("wq", wwide.at[0], wwide_v.at[0])
    load_wide("gq", gq, gq_v)
    load("win3", win.at[3], win_v.at[pl.ds(4 * PR, PR)])
    load_wide("xc", xc, xc_v)
    load("wo", wwide.at[1], wwide_v.at[1])
    load_wide("go", go, go_v)

    barrier = pltpu.get_barrier_semaphore()

    for d in range(1, EXN):
        pl.semaphore_signal(barrier, inc=1, device_id={"ex": (ex + d) % EXN}, device_id_type=MESH)
    for i in FAR_FIRST:
        pl.semaphore_signal(barrier, inc=1, device_id={"feat": ahead(i)}, device_id_type=MESH)

    def halves(x):
        high = x.astype(BF)
        return high, (x - high.astype(F32)).astype(BF)

    ready("hes", "qry")

    @pl.loop(0, 4)
    def _(m):
        q_high, q_low = halves(qry_v[:, m, :])
        h_high, h_low = halves(hes_v[m])
        hb_v[m] = h_high
        both = jnp.dot(
            jnp.concatenate([q_high, q_low], axis=0), h_high, preferred_element_type=F32
        )
        rest = jnp.dot(q_high, h_low, preferred_element_type=F32)
        ploc[m] = (both[0:QL] + (both[QL:2 * QL] + rest)).astype(BF)

    my_q = pl.ds(pl.multiple_of(ex * QL, QL), QL)

    def enter():
        pl.semaphore_wait(barrier, OWN - 1 + EXN - 1)

        @pl.loop(0, EXN - 1)
        def _(s):
            to = jnp.where(s < ex, s, s + 1)
            pltpu.make_async_remote_copy(
                src_ref=ploc, dst_ref=pall.at[:, my_q, :], send_sem=p_send, recv_sem=p_recv,
                device_id={"ex": to},
                device_id_type=MESH,
            ).start()

    late = ex >= EXN // 2
    pall[:, my_q, :] = ploc[...]

    half = lax.broadcasted_iota(jnp.int32, (128, 128), 1) < PR

    def rows_of(k):
        return pl.ds(pl.multiple_of(k * EXD, EXD), EXD)

    def project(m, target_v, weight, c, rows):
        o_t = lax.dot_general(
            weight[...], target_v[rows, :], NT, preferred_element_type=F32
        )
        count = o_t.shape[1] // 128
        for b in range(count):
            ot[m, c * count + b] = o_t[:, b * 128:(b + 1) * 128]

    def split(x, left, twice):
        turned = x if twice else pltpu.roll(x, PR, axis=1)
        on_left, on_right = (x, turned) if left else (turned, x)
        return jnp.where(half, on_left, 0.0).astype(BF), jnp.where(half, 0.0, on_right).astype(BF)

    def pair(m, g):
        rows = pl.ds(g * 128, 128)
        if m == QUERY:
            return split(pin[rows, 0:128], True, False)
        if m == KEY:
            return split(pin[rows, 0:128], False, False)
        if m == VALUE:
            return split(pin[rows, 128:256], True, True)
        return split(pin_o[rows, :], True, True)

    def outer(m, g):
        parts = [
            [ot[m, g, pl.ds(2 * ih + il, 16, stride=4), :].astype(BF) for il in range(2)]
            for ih in range(2)
        ]
        lhs = jnp.concatenate([jnp.concatenate(p, axis=1) for p in parts], axis=0)
        blocks = []
        for e in range(4):
            mk = mask_v[4 * g + e]
            blocks.append(lhs * jnp.concatenate([mk, mk], axis=0))
        lhs = jnp.concatenate(blocks, axis=0)
        rhs = jnp.concatenate(pair(m, g), axis=0)
        r = jnp.dot(lhs, rhs, preferred_element_type=F32)
        for e in range(4):
            for ih in range(2):
                at = (2 * e + ih) * 16
                g32[m, ih, pl.ds(4 * g + e, 16, stride=PITCH), :] = r[at:at + 16, :]

    def gather(m):
        for k in range(OWN):
            gsend[m, k * EXD:(k + 1) * EXD, :] = jnp.concatenate(
                [g32[m, ih, k * PITCH:k * PITCH + EXD, :] for ih in range(2)], axis=1
            ).astype(BF)

    def send(m):
        for i in FAR_FIRST:
            to = ahead(i)
            pltpu.make_async_remote_copy(
                src_ref=gsend.at[m, rows_of(to), :],
                dst_ref=grec.at[m, pl.ds(i * EXD, EXD), :],
                send_sem=g_send, recv_sem=g_recv.at[m if m < OUTPUT else OUTPUT + GROUP_OF[i]],
                device_id={"feat": to}, device_id_type=MESH,
            ).start()
        grec[m, 0:EXD, :] = gsend[m, rows_of(ft), :]

    def project_in(dst, source_v, weight, rows):
        dst[rows, :] = lax.dot_general(
            source_v[rows, :], weight[...], NT, preferred_element_type=F32
        )

    every = pl.ds(0, ROWS)
    ready("len")
    lane = lax.broadcasted_iota(jnp.int32, (16, 256), 1)
    lane_e = (lane // LEN) % 4
    lane_t = lane % LEN

    @pl.loop(0, EXD)
    def _(e):
        on = (lane_e == e % 4) & (lane_t < len_ref[e])
        mask_v[e] = jnp.where(on, 1.0, 0.0).astype(BF)

    ready("wnar", "gk", "gv")
    project(KEY, gk_v, wnar_v.at[0], 0, every)
    project(VALUE, gv_v, wnar_v.at[1], 0, every)
    pl.when(late)(enter)
    ready("win0", "win1", "win2")
    win_v[3 * PR:4 * PR, :] = win_v[2 * PR:3 * PR, :]
    over_chunks("xa", xa, xa_v, lambda c, rows: project_in(pin, xa_v, win_v.at[0:4 * PR], rows))
    pl.when(jnp.logical_not(late))(enter)
    for m in (KEY, VALUE):
        for g in range(EXD // 4):
            outer(m, g)
        gather(m)
        send(m)
    ready("wq")
    all_rows_of("gq", lambda c, rows: project(QUERY, gq_v, wwide_v.at[0], c, rows))
    for g in range(EXD // 4):
        outer(QUERY, g)
    gather(QUERY)
    send(QUERY)
    ready("win3")
    win_v[5 * PR:6 * PR, :] = win_v[4 * PR:5 * PR, :]
    all_rows_of("xc", lambda c, rows: project_in(pin_o, xc_v, win_v.at[4 * PR:6 * PR], rows))
    ready("wo")
    over_chunks("go", go, go_v, lambda c, rows: project(OUTPUT, go_v, wwide_v.at[1], c, rows))
    for g in range(EXD // 4):
        outer(OUTPUT, g)
    gather(OUTPUT)
    send(OUTPUT)

    others = (OWN - 1) * EXD

    def raw_part(m, rows):
        return lax.dot_general(grec[m, rows, :], pall[m], NT, preferred_element_type=F32)

    def self_part(m, rows):
        got = grec[m, rows, :]
        own = jnp.dot(got, hb_v[m], preferred_element_type=F32) * got.astype(F32)
        return own[:, 0:128] + own[:, 128:256]

    early = (KEY, VALUE, QUERY)
    all_rows = slice(0, OWN * EXD)
    for m in early:
        arrived(grec.at[m, pl.ds(0, others), :], g_recv.at[m])
        own = self_part(m, all_rows)
        tacc[...] = own if m == KEY else tacc[...] + own
    arrived(pall.at[:, pl.ds(0, QN - QL), :], p_recv)
    for m in early:
        raw = raw_part(m, all_rows)
        acc[...] = raw if m == KEY else acc[...] + raw

    for n, group in enumerate(GROUPS):
        partners = [i for i in group if i > 0]
        arrived(grec.at[OUTPUT, pl.ds(0, len(partners) * EXD), :], g_recv.at[OUTPUT + n])
    raw = raw_part(OUTPUT, all_rows) + acc[...]
    own = self_part(OUTPUT, all_rows) + tacc[...]
    own = own + pltpu.roll(own, 64, axis=1)
    high = own.astype(BF).astype(F32)
    left = lax.broadcasted_iota(jnp.int32, own.shape, 1) < 64
    sbuf[:, 0:QN] = raw.astype(BF)
    sbuf[:, QN:W] = jnp.where(left, high, own - high).astype(BF)
    for i in FAR_FIRST:
        at = pl.ds(i * EXD, EXD)
        pltpu.make_async_remote_copy(
            src_ref=sbuf.at[at, :], dst_ref=srec.at[at, :], send_sem=s_send,
            recv_sem=s_recv.at[GROUP_OF[i]], device_id={"feat": behind(i)}, device_id_type=MESH,
        ).start()

    total = sbuf[0:EXD, :].astype(F32)
    for n, group in enumerate(GROUPS):
        partners = [i for i in group if i > 0]
        arrived(srec.at[pl.ds(0, len(partners) * EXD), :], s_recv.at[n])
        for i in partners:
            total = total + srec[i * EXD:(i + 1) * EXD, :].astype(F32)
    self_inf = jnp.sum(total[:, QN:W], axis=1, keepdims=True)
    out_ref[...] = total[:, 0:QN] * lax.rsqrt(self_inf + 1e-06)

    arrived(gsend.at[:, pl.ds(0, others), :], g_send)
    arrived(sbuf.at[pl.ds(0, others), :], s_send)
    arrived(pall.at[:, pl.ds(0, QN - QL), :], p_send)


def per_device(
    lengths, attn_in, context, grad_q, grad_k, grad_v, grad_o,
    proj_in, proj_out_wide, proj_out_narrow, inv_hessian, query_feats,
):
    def flat(x):
        return x.reshape(ROWS, x.shape[-1])

    any_space = pl.BlockSpec(memory_space=pl.ANY)
    dma = pltpu.SemaphoreType.DMA
    return pl.pallas_call(
        kernel,
        out_shape=pltpu.VMEM((EXD, QN), F32),
        in_specs=[any_space] * 12,
        out_specs=pl.BlockSpec(memory_space=pltpu.VMEM),
        scratch_shapes=[
            pltpu.SMEM((EXD,), jnp.int32),
            pltpu.VMEM((ROWS, D), BF),
            pltpu.VMEM((ROWS, D), BF),
            pltpu.VMEM((ROWS, D), BF),
            pltpu.VMEM((ROWS, KVW), BF),
            pltpu.VMEM((ROWS, KVW), BF),
            pltpu.VMEM((ROWS, D), BF),
            pltpu.VMEM((6 * PR, D), BF),
            pltpu.VMEM((2, PR, D), BF),
            pltpu.VMEM((2, PR, KVW), BF),
            pltpu.VMEM((4, HB, HB), F32),
            pltpu.VMEM((QL, 4, HB), F32),
            pltpu.VMEM((4, HB, HB), BF),
            pltpu.VMEM((4, QL, HB), BF),
            pltpu.VMEM((4, QN, HB), BF),
            pltpu.VMEM((ROWS, 256), F32),
            pltpu.VMEM((ROWS, 128), F32),
            pltpu.VMEM((4, EXD // 4, PR, 128), F32),
            pltpu.VMEM((EXD, 16, 256), BF),
            pltpu.VMEM((4, 2, OWN * PITCH, 128), F32),
            pltpu.VMEM((4, OWN * EXD, HB), BF),
            pltpu.VMEM((4, OWN * EXD, HB), BF),
            pltpu.VMEM((OWN * EXD, QN), F32),
            pltpu.VMEM((OWN * EXD, 128), F32),
            pltpu.VMEM((OWN * EXD, W), BF),
            pltpu.VMEM((OWN * EXD, W), BF),
            dma((20,)),
            dma,
            dma,
            dma,
            dma((OUTPUT + len(GROUPS),)),
            dma,
            dma((len(GROUPS),)),
        ],
        compiler_params=pltpu.CompilerParams(
            collective_id=0, has_side_effects=True, vmem_limit_bytes=56 << 20
        ),
    )(
        lengths, flat(attn_in), flat(context), flat(grad_q), flat(grad_k), flat(grad_v),
        flat(grad_o), proj_in, proj_out_wide, proj_out_narrow, inv_hessian, query_feats,
    )


def solution(mesh):
    both = P(("ex", "feat"), None, None)
    in_specs = (
        P(("ex", "feat")), both, both, both, both, both, both,
        P(), P(), P(),
        P(None, "feat", None, None),
        P("ex", None, "feat"),
    )
    return jax.shard_map(
        per_device, mesh=mesh, in_specs=in_specs, out_specs=P(("ex", "feat"), None), check_vma=False
    )
```

```python
import jax
import jax.numpy as jnp
from jax import lax
from jax.experimental import pallas as pl
from jax.experimental.pallas import tpu as pltpu
from jax.sharding import PartitionSpec as P

MESH = pl.DeviceIdType.MESH
NT = (((1,), (1,)), ((), ()))
BF = jnp.bfloat16
F32 = jnp.float32

D = 4096
KVW = 1024
PR = 64
HB = 256
LEN = 32
EXD = 16
ROWS = EXD * LEN
SIDE = 4
OWN = SIDE * SIDE
EXN = 8
QL = 32
QN = 256
W = 384
RC = 256
PITCH = 17
QUERY, KEY, VALUE, OUTPUT = range(4)


def hops(s):
    dy, dx = divmod(s, SIDE)
    return min(dy, SIDE - dy) + min(dx, SIDE - dx)


SLOTS = sorted(range(OWN), key=hops)
GROUPS = [[i for i in range(OWN) if max(hops(SLOTS[i]), 1) == h] for h in range(1, SIDE + 1)]
GROUP_OF = {i: n for n, g in enumerate(GROUPS) for i in g}
FAR_FIRST = range(OWN - 1, 0, -1)


def arrived(ref, sem):
    pltpu.make_async_copy(ref, ref, sem).wait()


def kernel(
    lengths, xa, xc, gq, gk, gv, go, win, wwide, wnar, hes, qry, out_ref,
    len_ref, xa_v, xc_v, gq_v, gk_v, gv_v, go_v, win_v, wwide_v, wnar_v, hes_v, qry_v,
    hb_v, ploc, pall, pin, pin_o, ot, mask_v, g32, gsend, grec, acc, tacc, sbuf, srec,
    load_sem, p_send, p_recv, g_send, g_recv, s_send, s_recv,
):
    ex = lax.axis_index("ex")
    ft = lax.axis_index("feat")
    xs = [(ft % SIDE + d) % SIDE for d in range(SIDE)]
    ys = [((ft // SIDE + d) % SIDE) * SIDE for d in range(SIDE)]

    def ahead(i):
        dy, dx = divmod(SLOTS[i], SIDE)
        return ys[dy] + xs[dx]

    def behind(i):
        dy, dx = divmod(SLOTS[i], SIDE)
        return ys[-dy % SIDE] + xs[-dx % SIDE]

    loads = {}

    def load(name, src, dst):
        copy = pltpu.make_async_copy(src, dst, load_sem.at[len(loads)])
        copy.start()
        loads[name] = copy

    def ready(*names):
        for name in names:
            loads[name].wait()

    first_sem = {}

    def load_wide(name, src, dst):
        first_sem[name] = len(loads)
        for c in range(ROWS // RC):
            rows = pl.ds(c * RC, RC)
            load(f"{name}{c}", src.at[rows, :], dst.at[rows, :])

    def all_rows_of(name, body):
        ready(f"{name}0", f"{name}1")
        body(0, pl.ds(0, ROWS))

    def over_chunks(name, src, dst, body):
        @pl.loop(0, ROWS // RC)
        def _(c):
            rows = pl.ds(pl.multiple_of(c * RC, RC), RC)
            pltpu.make_async_copy(
                src.at[rows, :], dst.at[rows, :], load_sem.at[first_sem[name] + c]
            ).wait()
            body(c, rows)

    load("len", lengths, len_ref)
    load("hes", hes.at[:, 0], hes_v)
    load("qry", qry, qry_v)
    load("wnar", wnar, wnar_v)
    load("gk", gk, gk_v)
    load("gv", gv, gv_v)
    for m in range(3):
        load(f"win{m}", win.at[m], win_v.at[pl.ds(m * PR, PR)])
    load_wide("xa", xa, xa_v)
    load("wq", wwide.at[0], wwide_v.at[0])
    load_wide("gq", gq, gq_v)
    load("win3", win.at[3], win_v.at[pl.ds(4 * PR, PR)])
    load_wide("xc", xc, xc_v)
    load("wo", wwide.at[1], wwide_v.at[1])
    load_wide("go", go, go_v)

    barrier = pltpu.get_barrier_semaphore()

    for d in range(1, EXN):
        pl.semaphore_signal(barrier, inc=1, device_id={"ex": (ex + d) % EXN}, device_id_type=MESH)
    for i in FAR_FIRST:
        pl.semaphore_signal(barrier, inc=1, device_id={"feat": ahead(i)}, device_id_type=MESH)

    def halves(x):
        high = x.astype(BF)
        return high, (x - high.astype(F32)).astype(BF)

    ready("hes", "qry")

    @pl.loop(0, 4)
    def _(m):
        q_high, q_low = halves(qry_v[:, m, :])
        h_high, h_low = halves(hes_v[m])
        hb_v[m] = h_high
        both = jnp.dot(
            jnp.concatenate([q_high, q_low], axis=0), h_high, preferred_element_type=F32
        )
        rest = jnp.dot(q_high, h_low, preferred_element_type=F32)
        ploc[m] = (both[0:QL] + (both[QL:2 * QL] + rest)).astype(BF)

    my_q = pl.ds(pl.multiple_of(ex * QL, QL), QL)

    def enter():
        pl.semaphore_wait(barrier, OWN - 1 + EXN - 1)

        @pl.loop(0, EXN - 1)
        def _(s):
            to = jnp.where(s < ex, s, s + 1)
            pltpu.make_async_remote_copy(
                src_ref=ploc, dst_ref=pall.at[:, my_q, :], send_sem=p_send, recv_sem=p_recv,
                device_id={"ex": to},
                device_id_type=MESH,
            ).start()

    late = ex >= EXN // 2
    pall[:, my_q, :] = ploc[...]

    half = lax.broadcasted_iota(jnp.int32, (128, 128), 1) < PR

    def rows_of(k):
        return pl.ds(pl.multiple_of(k * EXD, EXD), EXD)

    def project(m, target_v, weight, c, rows):
        o_t = lax.dot_general(
            weight[...], target_v[rows, :], NT, preferred_element_type=F32
        )
        count = o_t.shape[1] // 128
        for b in range(count):
            ot[m, c * count + b, 0:PR, :] = o_t[:, b * 128:(b + 1) * 128]

    def split(x, left, twice):
        turned = x if twice else pltpu.roll(x, PR, axis=1)
        on_left, on_right = (x, turned) if left else (turned, x)
        return jnp.where(half, on_left, 0.0).astype(BF), jnp.where(half, 0.0, on_right).astype(BF)

    def pair(m, g):
        rows = pl.ds(g * 128, 128)
        if m == QUERY:
            return split(pin[rows, 0:128], True, False)
        if m == KEY:
            return split(pin[rows, 0:128], False, False)
        if m == VALUE:
            return split(pin[rows, 128:256], True, True)
        return split(pin_o[rows, :], True, True)

    def outer(m, g):
        parts = [
            [ot[m, g, pl.ds(2 * ih + il, 16, stride=4), :].astype(BF) for il in range(2)]
            for ih in range(2)
        ]
        lhs = jnp.concatenate([jnp.concatenate(p, axis=1) for p in parts], axis=0)
        blocks = []
        for e in range(4):
            mk = mask_v[4 * g + e]
            blocks.append(lhs * jnp.concatenate([mk, mk], axis=0))
        lhs = jnp.concatenate(blocks, axis=0)
        rhs = jnp.concatenate(pair(m, g), axis=0)
        r = jnp.dot(lhs, rhs, preferred_element_type=F32)
        for e in range(4):
            for ih in range(2):
                at = (2 * e + ih) * 16
                g32[m, ih, pl.ds(4 * g + e, 16, stride=PITCH), :] = r[at:at + 16, :]

    def gather(m):
        for k in range(OWN):
            gsend[m, k * EXD:(k + 1) * EXD, :] = jnp.concatenate(
                [g32[m, ih, k * PITCH:k * PITCH + EXD, :] for ih in range(2)], axis=1
            ).astype(BF)

    def send(m):
        for i in FAR_FIRST:
            to = ahead(i)
            pltpu.make_async_remote_copy(
                src_ref=gsend.at[m, rows_of(to), :],
                dst_ref=grec.at[m, pl.ds(i * EXD, EXD), :],
                send_sem=g_send, recv_sem=g_recv.at[m if m < OUTPUT else OUTPUT + GROUP_OF[i]],
                device_id={"feat": to}, device_id_type=MESH,
            ).start()
        grec[m, 0:EXD, :] = gsend[m, rows_of(ft), :]

    def project_in(dst, source_v, weight, rows):
        dst[rows, :] = lax.dot_general(
            source_v[rows, :], weight[...], NT, preferred_element_type=F32
        )

    every = pl.ds(0, ROWS)
    ready("len")
    lane = lax.broadcasted_iota(jnp.int32, (16, 256), 1)
    lane_e = (lane // LEN) % 4
    lane_t = lane % LEN

    @pl.loop(0, EXD)
    def _(e):
        on = (lane_e == e % 4) & (lane_t < len_ref[e])
        mask_v[e] = jnp.where(on, 1.0, 0.0).astype(BF)

    ready("wnar", "gk", "gv")
    project(KEY, gk_v, wnar_v.at[0], 0, every)
    project(VALUE, gv_v, wnar_v.at[1], 0, every)
    pl.when(late)(enter)
    ready("win0", "win1", "win2")
    win_v[3 * PR:4 * PR, :] = win_v[2 * PR:3 * PR, :]
    over_chunks("xa", xa, xa_v, lambda c, rows: project_in(pin, xa_v, win_v.at[0:4 * PR], rows))
    pl.when(jnp.logical_not(late))(enter)
    for m in (KEY, VALUE):
        for g in range(EXD // 4):
            outer(m, g)
        gather(m)
        send(m)
    ready("wq")
    all_rows_of("gq", lambda c, rows: project(QUERY, gq_v, wwide_v.at[0], c, rows))
    for g in range(EXD // 4):
        outer(QUERY, g)
    gather(QUERY)
    send(QUERY)
    ready("win3")
    win_v[5 * PR:6 * PR, :] = win_v[4 * PR:5 * PR, :]
    all_rows_of("xc", lambda c, rows: project_in(pin_o, xc_v, win_v.at[4 * PR:6 * PR], rows))
    ready("wo")
    over_chunks("go", go, go_v, lambda c, rows: project(OUTPUT, go_v, wwide_v.at[1], c, rows))
    for g in range(EXD // 4):
        outer(OUTPUT, g)
    gather(OUTPUT)
    send(OUTPUT)

    others = (OWN - 1) * EXD

    def raw_part(m, rows):
        return lax.dot_general(grec[m, rows, :], pall[m], NT, preferred_element_type=F32)

    def self_part(m, rows):
        got = grec[m, rows, :]
        own = jnp.dot(got, hb_v[m], preferred_element_type=F32) * got.astype(F32)
        return own[:, 0:128] + own[:, 128:256]

    early = (KEY, VALUE, QUERY)
    all_rows = slice(0, OWN * EXD)
    for m in early:
        arrived(grec.at[m, pl.ds(0, others), :], g_recv.at[m])
        own = self_part(m, all_rows)
        tacc[...] = own if m == KEY else tacc[...] + own
    arrived(pall.at[:, pl.ds(0, QN - QL), :], p_recv)
    for m in early:
        raw = raw_part(m, all_rows)
        acc[...] = raw if m == KEY else acc[...] + raw

    for n, group in enumerate(GROUPS):
        partners = [i for i in group if i > 0]
        arrived(grec.at[OUTPUT, pl.ds(0, len(partners) * EXD), :], g_recv.at[OUTPUT + n])
    raw = raw_part(OUTPUT, all_rows) + acc[...]
    own = self_part(OUTPUT, all_rows) + tacc[...]
    own = own + pltpu.roll(own, 64, axis=1)
    high = own.astype(BF).astype(F32)
    left = lax.broadcasted_iota(jnp.int32, own.shape, 1) < 64
    sbuf[:, 0:QN] = raw.astype(BF)
    sbuf[:, QN:W] = jnp.where(left, high, own - high).astype(BF)
    for i in FAR_FIRST:
        at = pl.ds(i * EXD, EXD)
        pltpu.make_async_remote_copy(
            src_ref=sbuf.at[at, :], dst_ref=srec.at[at, :], send_sem=s_send,
            recv_sem=s_recv.at[GROUP_OF[i]], device_id={"feat": behind(i)}, device_id_type=MESH,
        ).start()

    total = sbuf[0:EXD, :].astype(F32)
    for n, group in enumerate(GROUPS):
        partners = [i for i in group if i > 0]
        arrived(srec.at[pl.ds(0, len(partners) * EXD), :], s_recv.at[n])
        for i in partners:
            total = total + srec[i * EXD:(i + 1) * EXD, :].astype(F32)
    self_inf = jnp.sum(total[:, QN:W], axis=1, keepdims=True)
    out_ref[...] = total[:, 0:QN] * lax.rsqrt(self_inf + 1e-06)

    arrived(gsend.at[:, pl.ds(0, others), :], g_send)
    arrived(sbuf.at[pl.ds(0, others), :], s_send)
    arrived(pall.at[:, pl.ds(0, QN - QL), :], p_send)


def per_device(
    lengths, attn_in, context, grad_q, grad_k, grad_v, grad_o,
    proj_in, proj_out_wide, proj_out_narrow, inv_hessian, query_feats,
):
    def flat(x):
        return x.reshape(ROWS, x.shape[-1])

    any_space = pl.BlockSpec(memory_space=pl.ANY)
    dma = pltpu.SemaphoreType.DMA
    return pl.pallas_call(
        kernel,
        out_shape=pltpu.VMEM((EXD, QN), F32),
        in_specs=[any_space] * 12,
        out_specs=pl.BlockSpec(memory_space=pltpu.VMEM),
        scratch_shapes=[
            pltpu.SMEM((EXD,), jnp.int32),
            pltpu.VMEM((ROWS, D), BF),
            pltpu.VMEM((ROWS, D), BF),
            pltpu.VMEM((ROWS, D), BF),
            pltpu.VMEM((ROWS, KVW), BF),
            pltpu.VMEM((ROWS, KVW), BF),
            pltpu.VMEM((ROWS, D), BF),
            pltpu.VMEM((6 * PR, D), BF),
            pltpu.VMEM((2, PR, D), BF),
            pltpu.VMEM((2, PR, KVW), BF),
            pltpu.VMEM((4, HB, HB), F32),
            pltpu.VMEM((QL, 4, HB), F32),
            pltpu.VMEM((4, HB, HB), BF),
            pltpu.VMEM((4, QL, HB), BF),
            pltpu.VMEM((4, QN, HB), BF),
            pltpu.VMEM((ROWS, 256), F32),
            pltpu.VMEM((ROWS, 128), F32),
            pltpu.VMEM((4, EXD // 4, PR + 8, 128), F32),
            pltpu.VMEM((EXD, 16, 256), BF),
            pltpu.VMEM((4, 2, OWN * PITCH + 16, 128), F32),
            pltpu.VMEM((4, OWN * EXD, HB), BF),
            pltpu.VMEM((4, OWN * EXD, HB), BF),
            pltpu.VMEM((OWN * EXD, QN), F32),
            pltpu.VMEM((OWN * EXD, 128), F32),
            pltpu.VMEM((OWN * EXD, W), BF),
            pltpu.VMEM((OWN * EXD, W), BF),
            dma((20,)),
            dma,
            dma,
            dma,
            dma((OUTPUT + len(GROUPS),)),
            dma,
            dma((len(GROUPS),)),
        ],
        compiler_params=pltpu.CompilerParams(
            collective_id=0, has_side_effects=True, vmem_limit_bytes=56 << 20
        ),
    )(
        lengths, flat(attn_in), flat(context), flat(grad_q), flat(grad_k), flat(grad_v),
        flat(grad_o), proj_in, proj_out_wide, proj_out_narrow, inv_hessian, query_feats,
    )


def solution(mesh):
    both = P(("ex", "feat"), None, None)
    in_specs = (
        P(("ex", "feat")), both, both, both, both, both, both,
        P(), P(), P(),
        P(None, "feat", None, None),
        P("ex", None, "feat"),
    )
    return jax.shard_map(
        per_device, mesh=mesh, in_specs=in_specs, out_specs=P(("ex", "feat"), None), check_vma=False
    )
```
